32 devices in a mesh: ctx: 8 (over z, x), wa: 4 (over y, core).
Axes of the slice: x: 2, y: 2, z: 4, core: 2. Of those that a mesh axis runs over, the one named last changes fastest.
Arguments:
- x_in: bfloat16 [4, 1024, 1024], P('wa', 'ctx'), may hold values from -6 to 6
- seg_ids: int32 [4, 1024], P('wa'), may hold values from 0 to 2, never falling along the last dimension, each value on 1 to 512 neighbouring positions
- d_out: bfloat16 [4, 1024, 1024], P('wa', 'ctx'), may hold values from -6 to 6
- gain_in: float32 [1024], replicated, may hold values from 0.5 to 1.5
- w_mix_in: bfloat16 [1024, 4120], P(None, 'wa'), may hold values from -0.30078125 to 0.30078125
- conv_w: float32 [4, 1792], replicated, may hold values from -3 to 3
- conv_b: float32 [1792], replicated, may hold values from -3 to 3
- dt_bias: float32 [24], replicated, may hold values from -3 to 1
- a_log: float32 [24], replicated, may hold values from -8 to 0
- d_skip: float32 [24], replicated, may hold values from 0.5 to 1.5
- gain_gate: float32 [1536], replicated, may hold values from 0.5 to 1.5
- w_mix_out: bfloat16 [2048, 1024], P(None, 'wa'), may hold values from -0.25 to 0.25
- gain_ff: float32 [1024], replicated, may hold values from 0.5 to 1.5
- w_gate_up: bfloat16 [1024, 4096], P(None, 'wa'), may hold values from -0.1875 to 0.1875
- w_down: bfloat16 [2048, 1024], P(None, 'wa'), may hold values from -0.1875 to 0.1875
Outputs:
- out_rows: bfloat16 [4, 1024, 1024], P('wa', 'ctx')
- x_grad: float32 [4, 1024, 1024], P('wa', 'ctx')
- gain_in_grad: float32 [1024], replicated
- w_mix_in_grad: float32 [1024, 4120], P('ctx', 'wa')
- conv_w_grad: float32 [4, 1792], replicated
- conv_b_grad: float32 [1792], replicated
- dt_bias_grad: float32 [24], replicated
- a_log_grad: float32 [24], replicated
- d_skip_grad: float32 [24], replicated
- gain_gate_grad: float32 [1536], replicated
- w_mix_out_grad: float32 [2048, 1024], P('ctx', 'wa')
- gain_ff_grad: float32 [1024], replicated
- w_gate_up_grad: float32 [1024, 4096], P('ctx', 'wa')
- w_down_grad: float32 [2048, 1024], P('ctx', 'wa')
The draws below stay inside these ranges and needn't reach their ends.
Inputs may be any that keep to these rules, and one draw needn't show every extreme that they name: `seg_ids`: in each stream the document numbers never fall, every document 0 to 2 is present with 1 to 512 positions, and one has exactly 512.
All inputs are finite; a program needn't handle non-finite values.
Results may differ from the reference program's by a relative error of at most 0.03.
Values may be sent and summed in bfloat16 or wider, within the bound.
A program may use at most 256 MiB of HBM per device.

```python
import math
from functools import partial
import jax
import jax.numpy as jnp
import numpy as np
from jax import lax

D = 1024
MHEADS = 24
KCONV = 4
QHEADS = 8
KVHEADS = 2
HEAD_DIM = 64
FF = 2048
BLK = 64
DOCS = 3
DI = 1536
XBC = 1792
IN = 4120
CATW = 2048
STREAM = 1024
STREAMS = 4
DOC_MOST = 512
N_CTX = 8


ALIGN_LIMIT = 0.3


def draw_x_in(key, part):
    values = jax.random.truncated_normal(key, -6.0, 6.0, (STREAMS, STREAM, D), jnp.float32)
    return values.astype(jnp.bfloat16)


def draw_w_mix_in(key, part):
    values = jax.random.truncated_normal(key, -6.0, 6.0, (D, IN), jnp.float32) * D ** (-0.5)
    values = jnp.clip(values, -ALIGN_LIMIT, ALIGN_LIMIT)
    return values.astype(jnp.bfloat16)


def block_scale(key, dims, cuts, low, high):
    factor_of, own = 1.0, jax.random.fold_in(key, 6)
    for position, shards_of in cuts:
        heights = jnp.exp(jax.random.uniform(jax.random.fold_in(own, position), (shards_of,), jnp.float32, low / len(cuts), high / len(cuts)))
        factor_of = factor_of * jnp.repeat(heights, dims[position] // shards_of).reshape([-1 if axis == position else 1 for axis in range(len(dims))])
    return factor_of


def profile(amount, total, most, skew):
    loads = [(1 << 20) // math.isqrt(grade ** skew) + 1 for grade in range(2, amount + 1)]
    rest, given = total - most - (amount - 1), [1] * (amount - 1)
    while rest > 0:
        free = [i for i in range(amount - 1) if given[i] < most]
        pool, left = sum([loads[i] for i in free]), rest
        for i in free:
            addition = min(most - given[i], max(1, left * loads[i] // pool), rest)
            given[i] = given[i] + addition
            rest = rest - addition
    return np.array([most] + given)


def ragged(rng, amount, total, reach, skew):
    if amount == 2:
        one = jax.random.randint(rng, (), max(1, total - reach), min(reach, total - 1) + 1)
        return jnp.stack([one, total - one])
    sizes = jnp.asarray(profile(amount, total, reach, skew), jnp.int32)
    pairs = (amount - 1) // 2
    source_of, taker = sizes[1:1 + 2 * pairs:2], sizes[2:2 + 2 * pairs:2]
    slack = jnp.minimum(source_of - 1, reach - taker)
    passed = jax.random.randint(jax.random.fold_in(rng, 1), (pairs,), 0, 1 << 20) % (slack + 1)
    sizes = sizes.at[1:1 + 2 * pairs:2].set(source_of - passed).at[2:2 + 2 * pairs:2].set(taker + passed)
    return sizes[jax.random.permutation(jax.random.fold_in(rng, 2), amount)]


def centred(own_key, shape, deviation, bound, shards=(), held_as=jnp.bfloat16):
    drawn = deviation * jax.random.normal(own_key, shape, jnp.float32)
    if shards:
        drawn = drawn * block_scale(own_key, shape, shards, -0.22, 0.18)
    return jnp.clip(drawn, -bound, bound).astype(held_as)


def setup_inputs(seed: int = 0) -> dict:
    key_list = jax.random.split(jax.random.key(seed), 16)
    return {
        "x_in": draw_x_in(jax.random.fold_in(key_list[15], 71), 0),
        "seg_ids": jax.vmap(lambda own: jnp.searchsorted(jnp.cumsum(ragged(own, DOCS, STREAM, DOC_MOST, 2)), jnp.arange(STREAM), side="right"))(jax.random.split(key_list[1], STREAMS)).reshape((STREAMS, STREAM)).astype(jnp.int32),
        "d_out": centred(key_list[2], (STREAMS, STREAM, D), 1.0, 6.0, ((0, 4), (1, 8))),
        "gain_in": jnp.clip(1.0 + 0.1 * jax.random.normal(key_list[3], (D,), jnp.float32), 0.5, 1.5),
        "w_mix_in": draw_w_mix_in(jax.random.fold_in(key_list[15], 71), 0),
        "conv_w": centred(key_list[5], (KCONV, XBC), KCONV ** -0.5, 3.0, (), jnp.float32),
        "conv_b": centred(key_list[6], (XBC,), 0.5, 3.0, (), jnp.float32),
        "dt_bias": jnp.clip(jax.random.uniform(key_list[7], (MHEADS,), jnp.float32, -3.0, 1.0), -3.0, 1.0),
        "a_log": jnp.clip(jax.random.uniform(key_list[8], (MHEADS,), jnp.float32, -8.0, 0.0), -8.0, 0.0),
        "d_skip": jnp.clip(jax.random.uniform(key_list[9], (MHEADS,), jnp.float32, 0.5, 1.5), 0.5, 1.5),
        "gain_gate": jnp.clip(1.0 + 0.1 * jax.random.normal(key_list[10], (DI,), jnp.float32), 0.5, 1.5),
        "w_mix_out": centred(key_list[11], (CATW, D), (CATW // 4) ** -0.5, 0.25, ((1, 4),)),
        "gain_ff": jnp.clip(1.0 + 0.1 * jax.random.normal(key_list[12], (D,), jnp.float32), 0.5, 1.5),
        "w_gate_up": centred(key_list[13], (D, 2 * FF), D ** -0.5, 0.1875, ((1, 4),)),
        "w_down": centred(key_list[14], (FF, D), (FF // 2) ** -0.5, 0.1875, ((1, 4),)),
    }


EPS = 1e-05
ROPE_BASE = 100000000000.0
HIGH = lax.Precision.HIGHEST

def norm_rows(values, gain):
    return values * lax.rsqrt(lax.optimization_barrier(jnp.mean(values * values, axis=-1, keepdims=True)) + EPS) * gain

def swiglu(mixed):
    half_size = mixed.shape[-1] // 2
    return jax.nn.silu(mixed[:, :half_size]) * mixed[:, half_size:]

def rotate(values, positions, direction):
    head_size = values.shape[-1]
    half_size = head_size // 2
    frequency = ROPE_BASE ** (-2.0 * jnp.arange(half_size, dtype=jnp.float32) / head_size)
    angles = positions.astype(jnp.float32)[:, None] * frequency[None, :]
    cosine = jnp.cos(angles)[:, None, :]
    sine_part = direction * jnp.sin(angles)[:, None, :]
    first_half = values[..., :half_size]
    second_half = values[..., half_size:]
    return jnp.concatenate([first_half * cosine - second_half * sine_part, second_half * cosine + first_half * sine_part], axis=-1)

def conv_rows(extended, seg_ext, conv_w, conv_b):
    conv_lag = conv_w.shape[0] - 1
    length = extended.shape[0] - conv_lag
    summed = jnp.zeros((length, extended.shape[1]), jnp.float32) + conv_b[None, :]
    for tap_index in range(conv_lag + 1):
        same_doc = (seg_ext[tap_index:tap_index + length] == seg_ext[conv_lag:]).astype(jnp.float32)
        summed = summed + conv_w[tap_index][None, :] * extended[tap_index:tap_index + length] * same_doc[:, None]
    return jax.nn.silu(summed)

def block_inputs(extended, seg_ext, raw_dt, conv_w, conv_b, dt_bias, a_log, inner_width):
    mixed = conv_rows(extended, seg_ext, conv_w, conv_b)
    length = mixed.shape[0]
    mamba_heads = dt_bias.shape[0]
    state_size = (mixed.shape[1] - inner_width) // 2
    inputs_x = mixed[:, :inner_width].reshape(length, mamba_heads, inner_width // mamba_heads)
    b_rows = mixed[:, inner_width:inner_width + state_size]
    c_rows = mixed[:, inner_width + state_size:]
    step_dt = jax.nn.softplus(raw_dt + dt_bias[None, :])
    log_decay = -step_dt * jnp.exp(a_log)[None, :]
    return (inputs_x, b_rows, c_rows, step_dt, log_decay)

def block_state(inputs_x, b_rows, step_dt, log_decay, seg_block, seg_before):
    cumulative = jnp.cumsum(log_decay, axis=0)
    keep_end = (seg_block == seg_block[-1]).astype(jnp.float32)
    weights = jnp.exp(cumulative[-1][None, :] - cumulative) * keep_end[:, None] * step_dt
    end_state = jnp.einsum('shp,sn->hpn', weights[:, :, None] * inputs_x, b_rows, precision=HIGH)
    decay_all = jnp.exp(cumulative[-1]) * (seg_block[-1] == seg_before).astype(jnp.float32)
    return (decay_all, end_state)

def block_output(inputs_x, b_rows, c_rows, step_dt, log_decay, d_skip, seg_block, seg_before, state_in):
    length = inputs_x.shape[0]
    cumulative = jnp.cumsum(log_decay, axis=0)
    lower_tri = jnp.arange(length)[:, None] >= jnp.arange(length)[None, :]
    allowed = lower_tri & (seg_block[:, None] == seg_block[None, :])
    across = cumulative.T
    exponent = jnp.where(allowed[None], across[:, :, None] - across[:, None, :], -jnp.inf)
    intersection = jnp.dot(c_rows, b_rows.T, precision=HIGH)
    mixing = jnp.exp(exponent) * intersection[None] * step_dt.T[:, None, :]
    inner_out = jnp.einsum('hts,shp->thp', mixing, inputs_x, precision=HIGH)
    carried = (seg_block == seg_before).astype(jnp.float32)
    from_state = jnp.einsum('tn,hpn->thp', c_rows, state_in, precision=HIGH) * (jnp.exp(cumulative) * carried[:, None])[:, :, None]
    return inner_out + from_state + d_skip[None, :, None] * inputs_x

def gated_norm(outputs, gate_rows, gain_gate):
    return norm_rows(outputs * jax.nn.silu(gate_rows), gain_gate)

def mamba_stream(segments, xbc_rows, raw_dt, gate_rows, conv_w, conv_b, dt_bias, a_log, d_skip, gain_gate):
    conv_lag = conv_w.shape[0] - 1
    inner_width = gain_gate.shape[0]
    length = xbc_rows.shape[0]
    block_count = length // BLK
    extended = jnp.concatenate([jnp.zeros((conv_lag, xbc_rows.shape[1]), jnp.float32), xbc_rows], axis=0)
    seg_ext = jnp.concatenate([jnp.full((conv_lag,), -1, jnp.int32), segments], axis=0)
    inputs_x, b_rows, c_rows, step_dt, log_decay = block_inputs(extended, seg_ext, raw_dt, conv_w, conv_b, dt_bias, a_log, inner_width)
    seg_prior = jnp.concatenate([segments[:1], segments[:-1]], axis=0)

    def blocks_of(array):
        return array.reshape((block_count, BLK) + array.shape[1:])
    elements = (blocks_of(inputs_x), blocks_of(b_rows), blocks_of(c_rows), blocks_of(step_dt), blocks_of(log_decay), blocks_of(segments), blocks_of(seg_prior)[:, 0])

    def advance(state_in, element):
        x_block, b_block, c_block, dt_block, log_block, seg_block, seg_first = element
        outputs = block_output(x_block, b_block, c_block, dt_block, log_block, d_skip, seg_block, seg_first, state_in)
        decay_all, end_state = block_state(x_block, b_block, dt_block, log_block, seg_block, seg_first)
        return (decay_all[:, None, None] * state_in + end_state, outputs)
    mamba_heads = dt_bias.shape[0]
    start_state = jnp.zeros((mamba_heads, inner_width // mamba_heads, b_rows.shape[1]), jnp.float32)
    final_state, outputs = lax.scan(advance, start_state, elements)
    return gated_norm(outputs.reshape(length, inner_width), gate_rows, gain_gate)

def attention_forward(q_rot, k_rot, v_rows, segments):
    length = q_rot.shape[0]
    query_rows = min(512, length)
    key_pos = jnp.arange(length, dtype=jnp.int32)
    score_scale = HEAD_DIM ** (-0.5)
    key_float = lax.optimization_barrier(k_rot).astype(jnp.float32)
    value_float = v_rows.astype(jnp.float32)

    def one_block(block_index):
        first_row = block_index * query_rows
        q_block = lax.dynamic_slice_in_dim(q_rot, first_row, query_rows, 0).astype(jnp.float32)
        seg_query = lax.dynamic_slice_in_dim(segments, first_row, query_rows, 0)
        query_pos = first_row + jnp.arange(query_rows, dtype=jnp.int32)
        allowed = (key_pos[None, :] <= query_pos[:, None]) & (segments[None, :] == seg_query[:, None])
        scores = jnp.einsum('tgjd,sgd->gjts', q_block, key_float) * score_scale
        row_max = lax.optimization_barrier(jnp.max(jnp.where(allowed, scores, -1e+30), axis=-1))
        row_total = lax.optimization_barrier(jnp.sum(jnp.where(allowed, jnp.exp(scores - row_max[..., None]), 0.0), axis=-1))
        log_total = row_max + jnp.log(row_total)
        probability = jnp.where(allowed, jnp.exp(scores - log_total[..., None]), 0.0).astype(jnp.bfloat16)
        prob_float = lax.optimization_barrier(probability).astype(jnp.float32)
        attended = jnp.einsum('gjts,sgd->tgjd', prob_float, value_float)
        return (attended.astype(jnp.bfloat16), log_total)
    attended, log_total = lax.map(one_block, jnp.arange(length // query_rows, dtype=jnp.int32))
    return (attended.reshape((length,) + q_rot.shape[1:]), log_total)

def attention_backward(q_rot, k_rot, v_rows, segments, attended, log_total, d_att):
    length = q_rot.shape[0]
    query_rows = min(512, length)
    key_pos = jnp.arange(length, dtype=jnp.int32)
    score_scale = HEAD_DIM ** (-0.5)
    key_float = k_rot.astype(jnp.float32)
    value_float = v_rows.astype(jnp.float32)
    d_term = lax.optimization_barrier(jnp.sum(d_att.astype(jnp.float32) * attended.astype(jnp.float32), axis=-1))

    def one_block(carry, block_index):
        key_grad, value_grad = carry
        first_row = block_index * query_rows
        q_block = lax.dynamic_slice_in_dim(q_rot, first_row, query_rows, 0).astype(jnp.float32)
        d_block = lax.dynamic_slice_in_dim(d_att, first_row, query_rows, 0).astype(jnp.float32)
        term_block = jnp.transpose(lax.dynamic_slice_in_dim(d_term, first_row, query_rows, 0), (1, 2, 0))
        seg_query = lax.dynamic_slice_in_dim(segments, first_row, query_rows, 0)
        query_pos = first_row + jnp.arange(query_rows, dtype=jnp.int32)
        allowed = (key_pos[None, :] <= query_pos[:, None]) & (segments[None, :] == seg_query[:, None])
        scores = jnp.einsum('tgjd,sgd->gjts', q_block, key_float) * score_scale
        probability = jnp.where(allowed, jnp.exp(scores - log_total[block_index][..., None]), 0.0)
        prob_round = lax.optimization_barrier(probability.astype(jnp.bfloat16)).astype(jnp.float32)
        d_prob = jnp.einsum('tgjd,sgd->gjts', d_block, value_float)
        d_score = lax.optimization_barrier((probability * (d_prob - term_block[..., None])).astype(jnp.bfloat16)).astype(jnp.float32)
        q_grad = jnp.einsum('gjts,sgd->tgjd', d_score, key_float) * score_scale
        key_grad = key_grad + jnp.einsum('gjts,tgjd->sgd', d_score, q_block) * score_scale
        value_grad = value_grad + jnp.einsum('gjts,tgjd->sgd', prob_round, d_block)
        return ((key_grad, value_grad), q_grad)
    zero_grad = jnp.zeros(k_rot.shape, jnp.float32)
    (key_grad, value_grad), q_grad = lax.scan(one_block, (zero_grad, zero_grad), jnp.arange(length // query_rows, dtype=jnp.int32))
    return (q_grad.reshape(q_rot.shape), key_grad, value_grad)

def to_natural(stored):
    tail_shape = stored.shape[1:]
    shaped = stored.reshape((N_CTX, 2, BLK) + tail_shape)
    return jnp.concatenate([shaped[:, 0].reshape((N_CTX * BLK,) + tail_shape), shaped[::-1, 1].reshape((N_CTX * BLK,) + tail_shape)], axis=0)

def to_stored(natural):
    tail_shape = natural.shape[1:]
    half_len = N_CTX * BLK
    leading = natural[:half_len].reshape((N_CTX, BLK) + tail_shape)
    trailing = natural[half_len:].reshape((N_CTX, BLK) + tail_shape)[::-1]
    return jnp.stack([leading, trailing], axis=1).reshape(natural.shape)

def reference(x_in, seg_ids, d_out, gain_in, w_mix_in, conv_w, conv_b, dt_bias, a_log, d_skip, gain_gate, w_mix_out, gain_ff, w_gate_up, w_down):
    inner_width = gain_gate.shape[0]
    conv_width = conv_w.shape[1]
    mamba_heads = dt_bias.shape[0]
    groups = QHEADS // KVHEADS
    length = STREAM
    positions = jnp.arange(length, dtype=jnp.int32)
    col_q = inner_width + conv_width + mamba_heads
    col_k = col_q + QHEADS * HEAD_DIM
    col_v = col_k + KVHEADS * HEAD_DIM

    def one_stream(grads, element):
        x_stored, segments, dy_stored = element
        x_rows = to_natural(x_stored).astype(jnp.float32)
        h_rows, norm_in_back = jax.vjp(norm_rows, x_rows, gain_in)
        h_bf = h_rows.astype(jnp.bfloat16)
        proj = jnp.dot(h_bf, w_mix_in, preferred_element_type=jnp.float32).astype(jnp.bfloat16)
        proj = lax.optimization_barrier(proj)
        gate_part = proj[:, :inner_width].astype(jnp.float32)
        xbc_part = proj[:, inner_width:inner_width + conv_width].astype(jnp.float32)
        raw_dt = proj[:, inner_width + conv_width:col_q].astype(jnp.float32)
        q_rot = rotate(proj[:, col_q:col_k].astype(jnp.float32).reshape(length, QHEADS, HEAD_DIM), positions, 1.0).astype(jnp.bfloat16)
        q_rot = lax.optimization_barrier(q_rot).reshape(length, KVHEADS, groups, HEAD_DIM)
        k_rot = rotate(proj[:, col_k:col_v].astype(jnp.float32).reshape(length, KVHEADS, HEAD_DIM), positions, 1.0).astype(jnp.bfloat16)
        v_rows = proj[:, col_v:].reshape(length, KVHEADS, HEAD_DIM)
        attended, log_total = attention_forward(q_rot, k_rot, v_rows, segments)
        mamba_out, mamba_back = jax.vjp(partial(mamba_stream, segments), xbc_part, raw_dt, gate_part, conv_w, conv_b, dt_bias, a_log, d_skip, gain_gate)
        joined = jnp.concatenate([mamba_out.astype(jnp.bfloat16), attended.reshape(length, -1)], axis=1)
        x_mid = x_rows + jnp.dot(joined, w_mix_out, preferred_element_type=jnp.float32)
        h2_rows, norm_ff_back = jax.vjp(norm_rows, x_mid, gain_ff)
        h2_bf = h2_rows.astype(jnp.bfloat16)
        gate_up = jnp.dot(h2_bf, w_gate_up, preferred_element_type=jnp.float32)
        act_rows, act_back = jax.vjp(swiglu, gate_up)
        act_bf = act_rows.astype(jnp.bfloat16)
        out_rows = (x_mid + jnp.dot(act_bf, w_down, preferred_element_type=jnp.float32)).astype(jnp.bfloat16)
        dy_bf = to_natural(dy_stored)
        d_act = jnp.dot(dy_bf, w_down.T, preferred_element_type=jnp.float32)
        g_down = jnp.dot(act_bf.T, dy_bf, preferred_element_type=jnp.float32)
        d_gate_up = act_back(d_act)[0].astype(jnp.bfloat16)
        d_h2 = jnp.dot(d_gate_up, w_gate_up.T, preferred_element_type=jnp.float32)
        g_gate_up = jnp.dot(h2_bf.T, d_gate_up, preferred_element_type=jnp.float32)
        d_mid, g_gain_ff = norm_ff_back(d_h2)
        d_mid = d_mid + dy_bf.astype(jnp.float32)
        d_mix = d_mid.astype(jnp.bfloat16)
        d_joined = jnp.dot(d_mix, w_mix_out.T, preferred_element_type=jnp.float32)
        g_mix_out = jnp.dot(joined.T, d_mix, preferred_element_type=jnp.float32)
        d_att = d_joined[:, inner_width:].astype(jnp.bfloat16).reshape(length, KVHEADS, groups, HEAD_DIM)
        q_grad, key_grad, value_grad = attention_backward(q_rot, k_rot, v_rows, segments, attended, log_total, d_att)
        d_q = rotate(q_grad.reshape(length, QHEADS, HEAD_DIM), positions, -1.0).reshape(length, -1)
        d_k = rotate(key_grad, positions, -1.0).reshape(length, -1)
        mamba_grads = mamba_back(d_joined[:, :inner_width])
        d_proj = jnp.concatenate([mamba_grads[2], mamba_grads[0], mamba_grads[1], d_q, d_k, value_grad.reshape(length, -1)], axis=1).astype(jnp.bfloat16)
        d_h = jnp.dot(d_proj, w_mix_in.T, preferred_element_type=jnp.float32)
        g_mix_in = jnp.dot(h_bf.T, d_proj, preferred_element_type=jnp.float32)
        d_x_norm, g_gain_in = norm_in_back(d_h)
        d_x = d_mid + d_x_norm
        new_grads = (grads[0] + g_gain_in, grads[1] + g_mix_in, grads[2] + mamba_grads[3], grads[3] + mamba_grads[4], grads[4] + mamba_grads[5], grads[5] + mamba_grads[6], grads[6] + mamba_grads[7], grads[7] + mamba_grads[8], grads[8] + g_mix_out, grads[9] + g_gain_ff, grads[10] + g_gate_up, grads[11] + g_down)
        return (new_grads, (to_stored(out_rows), to_stored(d_x)))
    params = (gain_in, w_mix_in, conv_w, conv_b, dt_bias, a_log, d_skip, gain_gate, w_mix_out, gain_ff, w_gate_up, w_down)
    zero_grads = tuple((jnp.zeros(param.shape, jnp.float32) for param in params))
    grads, (outs, x_grads) = lax.scan(one_stream, zero_grads, (x_in, seg_ids, d_out))
    return (outs, x_grads, grads[0], grads[1], grads[2], grads[3], grads[4], grads[5], grads[6], grads[7], grads[8], grads[9], grads[10], grads[11])
```

```python
import jax
import jax.numpy as jnp
from jax import lax
from jax.sharding import PartitionSpec as P

QHEADS = 8
KVHEADS = 2
HEAD_DIM = 64


EPS = 1e-05
ROPE_BASE = 100000000000.0
HIGH = lax.Precision.HIGHEST


def extended_2(cells, sides, width):
    for axis, dim in sides:
        count = lax.axis_size(axis)
        ends = count - 1
        head = lax.slice_in_dim(cells, 0, width, axis=dim)
        tail = lax.slice_in_dim(cells, cells.shape[dim] - width, cells.shape[dim], axis=dim)
        cells = jnp.concatenate(
            [
                lax.ppermute(tail, axis, [(i, (i + 1) % count) for i in range(ends)]),
                cells,
                lax.ppermute(head, axis, [((i + 1) % count, i) for i in range(ends)]),
            ],
            axis=dim,
        )
    return cells


def norm_rows(values, gain):
    return values * lax.rsqrt(jnp.mean(values * values, axis=-1, keepdims=True) + EPS) * gain


def swiglu(mixed):
    half_size = mixed.shape[-1] // 2
    return jax.nn.silu(mixed[:, :half_size]) * mixed[:, half_size:]


def rotate(values, positions, direction):
    head_size = values.shape[-1]
    half_size = head_size // 2
    frequency = ROPE_BASE ** (-2.0 * jnp.arange(half_size, dtype=jnp.float32) / head_size)
    angles = positions.astype(jnp.float32)[:, None] * frequency[None, :]
    cosine = jnp.cos(angles)[:, None, :]
    sine_part = direction * jnp.sin(angles)[:, None, :]
    first_half = values[..., :half_size]
    second_half = values[..., half_size:]
    return jnp.concatenate(
        [
            first_half * cosine - second_half * sine_part,
            second_half * cosine + first_half * sine_part,
        ],
        axis=-1,
    )


def conv_rows(extended, seg_ext, conv_w, conv_b):
    conv_lag = conv_w.shape[0] - 1
    length = extended.shape[0] - conv_lag
    summed = jnp.zeros((length, extended.shape[1]), jnp.float32) + conv_b[None, :]
    for tap_index in range(conv_lag + 1):
        same_doc = (seg_ext[tap_index : tap_index + length] == seg_ext[conv_lag:]).astype(
            jnp.float32
        )
        summed = (
            summed
            + conv_w[tap_index][None, :]
            * extended[tap_index : tap_index + length]
            * same_doc[:, None]
        )
    return jax.nn.silu(summed)


def block_inputs(extended, seg_ext, raw_dt, conv_w, conv_b, dt_bias, a_log, inner_width):
    mixed = conv_rows(extended, seg_ext, conv_w, conv_b)
    length = mixed.shape[0]
    mamba_heads = dt_bias.shape[0]
    state_size = (mixed.shape[1] - inner_width) // 2
    inputs_x = mixed[:, :inner_width].reshape(length, mamba_heads, inner_width // mamba_heads)
    b_rows = mixed[:, inner_width : inner_width + state_size]
    c_rows = mixed[:, inner_width + state_size :]
    step_dt = jax.nn.softplus(raw_dt + dt_bias[None, :])
    log_decay = -step_dt * jnp.exp(a_log)[None, :]
    return (inputs_x, b_rows, c_rows, step_dt, log_decay)


def block_state(inputs_x, b_rows, step_dt, log_decay, seg_block, seg_before):
    cumulative = jnp.cumsum(log_decay, axis=0)
    keep_end = (seg_block == seg_block[-1]).astype(jnp.float32)
    weights = jnp.exp(cumulative[-1][None, :] - cumulative) * keep_end[:, None] * step_dt
    end_state = jnp.einsum("shp,sn->hpn", weights[:, :, None] * inputs_x, b_rows, precision=HIGH)
    decay_all = jnp.exp(cumulative[-1]) * (seg_block[-1] == seg_before).astype(jnp.float32)
    return (decay_all, end_state)


def block_output(
    inputs_x, b_rows, c_rows, step_dt, log_decay, d_skip, seg_block, seg_before, state_in
):
    length = inputs_x.shape[0]
    cumulative = jnp.cumsum(log_decay, axis=0)
    lower_tri = jnp.arange(length)[:, None] >= jnp.arange(length)[None, :]
    allowed = lower_tri & (seg_block[:, None] == seg_block[None, :])
    across = cumulative.T
    exponent = jnp.where(allowed[None], across[:, :, None] - across[:, None, :], -jnp.inf)
    intersection = jnp.dot(c_rows, b_rows.T, precision=HIGH)
    mixing = jnp.exp(exponent) * intersection[None] * step_dt.T[:, None, :]
    inner_out = jnp.einsum("hts,shp->thp", mixing, inputs_x, precision=HIGH)
    carried = (seg_block == seg_before).astype(jnp.float32)
    from_state = (
        jnp.einsum("tn,hpn->thp", c_rows, state_in, precision=HIGH)
        * (jnp.exp(cumulative) * carried[:, None])[:, :, None]
    )
    return inner_out + from_state + d_skip[None, :, None] * inputs_x


def gated_norm(outputs, gate_rows, gain_gate):
    return norm_rows(outputs * jax.nn.silu(gate_rows), gain_gate)


def block_chain(states, decays, reverse):
    order = range(states.shape[0])
    order = order[::-1] if reverse else order
    held = jnp.zeros(states.shape[1:], jnp.float32)
    before = [None] * states.shape[0]
    for at in order:
        before[at] = held.astype(jnp.bfloat16)
        held = decays[at][:, None] * held + states[at].astype(jnp.float32)
    return jnp.stack(before)


def swap_blocks(parts):
    return jnp.concatenate([parts[:, 0], parts[::-1, 1]], axis=0)


def unswap_blocks(blocks, count):
    return jnp.stack([blocks[:count], blocks[count:][::-1]], axis=1)


def cut_rows(states, count):
    rows = states.shape[1] * states.shape[2] // count
    cut = states.astype(jnp.bfloat16).reshape(2, count, rows, states.shape[3])
    return jnp.swapaxes(cut, 0, 1)


def join_rows(cut, shape):
    return jnp.swapaxes(cut, 0, 1).reshape(shape).astype(jnp.float32)


def swap_axis(parts):
    return lax.all_to_all(parts, "ctx", split_axis=0, concat_axis=0, tiled=True)


def states_before(states, decays, ctx_count):
    heads, width, size = states.shape[1:]
    rows = heads * width // ctx_count
    cut = cut_rows(states, ctx_count)
    high = decays.astype(jnp.bfloat16)
    low = (decays - high.astype(jnp.float32)).astype(jnp.bfloat16)
    marks = jnp.pad(jnp.stack([high, low], axis=1), ((0, 0), (0, 14), (0, size - heads)))
    marks = jnp.broadcast_to(marks[None], (ctx_count,) + marks.shape)
    got = swap_axis(jnp.concatenate([cut, marks], axis=2))
    all_decays = (got[:, :, rows, :heads].astype(jnp.float32)) + got[:, :, rows + 1, :heads].astype(
        jnp.float32
    )
    all_decays = jnp.repeat(swap_blocks(all_decays), width, axis=1)
    my_decays = lax.dynamic_slice_in_dim(all_decays, lax.axis_index("ctx") * rows, rows, 1)
    before = block_chain(swap_blocks(got[:, :, :rows]), my_decays, False)
    back = swap_axis(unswap_blocks(before, ctx_count))
    return join_rows(back, states.shape), my_decays


def grads_after(grads, my_decays, ctx_count):
    got = swap_axis(cut_rows(grads, ctx_count))
    after = block_chain(swap_blocks(got), my_decays, True)
    return join_rows(swap_axis(unswap_blocks(after, ctx_count)), grads.shape)


def by_columns(values):
    return lax.all_to_all(values, "wa", split_axis=1, concat_axis=0, tiled=True)


def shares(values, count):
    return values.reshape(values.shape[0], count, values.shape[1] // count)


def by_columns_of(first, second, third, count):
    cuts = [shares(first, count), shares(second, count), shares(third, count)]
    joined = jnp.concatenate(cuts, axis=2)
    got = by_columns(joined.reshape(joined.shape[0], -1))
    one = cuts[0].shape[2]
    two = one + cuts[1].shape[2]
    return (got[:, :one], got[:, one:two], got[:, two:])


def column_grad(kept_rows, grad_cols):
    partial_grad = jnp.einsum("tk,tn->kn", kept_rows, grad_cols, preferred_element_type=jnp.float32)
    return lax.psum_scatter(
        partial_grad.astype(jnp.bfloat16), "ctx", scatter_dimension=0, tiled=True
    ).astype(jnp.float32)


def to_stored(natural, ctx_count):
    tail_shape = natural.shape[1:]
    half_len = natural.shape[0] // 2
    block_len = half_len // ctx_count
    leading = natural[:half_len].reshape((ctx_count, block_len) + tail_shape)
    trailing = natural[half_len:].reshape((ctx_count, block_len) + tail_shape)[::-1]
    return jnp.stack([leading, trailing], axis=1).reshape(natural.shape)


def local(
    x_in,
    seg_ids,
    d_out,
    gain_in,
    w_mix_in,
    conv_w,
    conv_b,
    dt_bias,
    a_log,
    d_skip,
    gain_gate,
    w_mix_out,
    gain_ff,
    w_gate_up,
    w_down,
):
    ctx_count = lax.axis_size("ctx")
    wa_count = lax.axis_size("wa")
    ctx_place = lax.axis_index("ctx")
    at_end = ctx_place == ctx_count - 1
    tokens = x_in[0]
    row_count = tokens.shape[0]
    block_len = row_count // 2
    seg_all = seg_ids[0]
    inner_width = gain_gate.shape[0]
    conv_width = conv_w.shape[1]
    mamba_heads = dt_bias.shape[0]
    conv_lag = conv_w.shape[0] - 1
    groups = QHEADS // KVHEADS
    score_scale = HEAD_DIM ** (-0.5)
    starts = (ctx_place * block_len, (2 * ctx_count - 1 - ctx_place) * block_len)
    offsets = jnp.arange(block_len, dtype=jnp.int32)
    positions = jnp.concatenate([starts[0] + offsets, starts[1] + offsets])
    x_rows = tokens.astype(jnp.float32)
    h_rows, norm_in_back = jax.vjp(norm_rows, x_rows, gain_in)
    h_all = lax.all_gather(h_rows.astype(jnp.bfloat16), "wa", axis=0, tiled=True)
    proj_cols = jnp.dot(h_all, w_mix_in, preferred_element_type=jnp.float32).astype(jnp.bfloat16)
    proj = lax.all_to_all(proj_cols, "wa", split_axis=0, concat_axis=1, tiled=True)
    proj = lax.optimization_barrier(proj)
    m_mix_out = lax.all_gather(w_mix_out, "wa", axis=1, tiled=True)
    m_down = lax.all_gather(w_down, "wa", axis=1, tiled=True)
    m_gate_up = lax.all_gather(w_gate_up, "wa", axis=1, tiled=True)
    col_q = inner_width + conv_width + mamba_heads
    col_k = col_q + QHEADS * HEAD_DIM
    col_v = col_k + KVHEADS * HEAD_DIM
    kv_width = KVHEADS * HEAD_DIM
    gate_part = proj[:, :inner_width].astype(jnp.float32)
    xbc_part = proj[:, inner_width : inner_width + conv_width]
    dt_part = proj[:, inner_width + conv_width : col_q].astype(jnp.float32)
    q_rot = rotate(
        proj[:, col_q:col_k].astype(jnp.float32).reshape(row_count, QHEADS, HEAD_DIM),
        positions,
        1.0,
    ).astype(jnp.bfloat16)
    q_rot = q_rot.reshape(row_count, KVHEADS, groups, HEAD_DIM)
    k_rot = rotate(
        proj[:, col_k:col_v].astype(jnp.float32).reshape(row_count, KVHEADS, HEAD_DIM),
        positions,
        1.0,
    ).astype(jnp.bfloat16)
    kv_all = lax.all_gather(
        jnp.concatenate([k_rot.reshape(row_count, kv_width), proj[:, col_v:]], axis=1),
        "ctx",
        axis=0,
        tiled=True,
    )
    tails = (xbc_part[block_len - conv_lag : block_len], xbc_part[row_count - conv_lag :])
    rim = extended_2(jnp.stack([tails[1], tails[0]]), (("ctx", 0),), 1)
    previous = (rim[0], jnp.where(at_end, tails[0], rim[3]))
    seg_exts = []
    seg_befores = []
    extendeds = []
    for part_index in range(2):
        low_row = part_index * block_len
        index_ext = (
            starts[part_index] - conv_lag + jnp.arange(block_len + conv_lag, dtype=jnp.int32)
        )
        seg_exts.append(jnp.where(index_ext >= 0, jnp.take(seg_all, jnp.maximum(index_ext, 0)), -1))
        seg_befores.append(jnp.take(seg_all, jnp.maximum(starts[part_index] - 1, 0)))
        extendeds.append(
            jnp.concatenate(
                [previous[part_index], xbc_part[low_row : low_row + block_len]], axis=0
            ).astype(jnp.float32)
        )
    seg_ext = jnp.stack(seg_exts)
    seg_before = jnp.stack(seg_befores)
    seg_block = seg_ext[:, conv_lag:]

    def all_inputs(extended, raw_dt, conv_w, conv_b, dt_bias, a_log):
        return jax.vmap(
            lambda ext, seg, raw: block_inputs(
                ext, seg, raw, conv_w, conv_b, dt_bias, a_log, inner_width
            )
        )(extended, seg_ext, raw_dt)

    def all_states(inputs_x, b_rows, step_dt, log_decay):
        return jax.vmap(block_state)(inputs_x, b_rows, step_dt, log_decay, seg_block, seg_before)

    def all_outputs(
        inputs_x, b_rows, c_rows, step_dt, log_decay, gate_rows, d_skip, gain_gate, state_in
    ):
        outputs = jax.vmap(block_output, in_axes=(0, 0, 0, 0, 0, None, 0, 0, 0))(
            inputs_x, b_rows, c_rows, step_dt, log_decay, d_skip, seg_block, seg_before, state_in
        )
        return gated_norm(outputs.reshape(row_count, inner_width), gate_rows, gain_gate)

    (inputs_x, b_rows, c_rows, step_dt, log_decay), inputs_back = jax.vjp(
        all_inputs,
        jnp.stack(extendeds),
        dt_part.reshape(2, block_len, mamba_heads),
        conv_w,
        conv_b,
        dt_bias,
        a_log,
    )
    (decays, states), states_back = jax.vjp(all_states, inputs_x, b_rows, step_dt, log_decay)
    incoming, my_decays = states_before(states, decays, ctx_count)

    keys = kv_all[:, :kv_width].reshape(-1, KVHEADS, HEAD_DIM)
    values = kv_all[:, kv_width:].reshape(-1, KVHEADS, HEAD_DIM)
    key_seg = to_stored(seg_all, ctx_count)
    key_pos = to_stored(jnp.arange(seg_all.shape[0], dtype=jnp.int32), ctx_count)
    query_seg = seg_block.reshape(row_count)
    allowed = (key_pos[None, :] <= positions[:, None]) & (key_seg[None, :] == query_seg[:, None])
    scores = (
        jnp.einsum("tgjd,sgd->gjts", q_rot, keys, preferred_element_type=jnp.float32) * score_scale
    )
    row_max = jnp.max(jnp.where(allowed, scores, -1e30), axis=-1, keepdims=True)
    raised = jnp.where(allowed, jnp.exp(scores - row_max), 0.0)
    probability = raised * (1.0 / jnp.sum(raised, axis=-1, keepdims=True))
    prob_bf = probability.astype(jnp.bfloat16)
    attended = jnp.einsum(
        "gjts,sgd->tgjd", prob_bf, values, preferred_element_type=jnp.float32
    ).astype(jnp.bfloat16)

    mamba_out, out_back = jax.vjp(
        all_outputs,
        inputs_x,
        b_rows,
        c_rows,
        step_dt,
        log_decay,
        gate_part,
        d_skip,
        gain_gate,
        incoming,
    )
    joined = jnp.concatenate(
        [mamba_out.astype(jnp.bfloat16), attended.reshape(row_count, QHEADS * HEAD_DIM)], axis=1
    )
    x_mid = x_rows + jnp.dot(joined, m_mix_out, preferred_element_type=jnp.float32)
    h2_rows, norm_ff_back = jax.vjp(norm_rows, x_mid, gain_ff)
    h2_bf = h2_rows.astype(jnp.bfloat16)
    gate_up = jnp.dot(h2_bf, m_gate_up, preferred_element_type=jnp.float32)
    act_rows, act_back = jax.vjp(swiglu, gate_up)
    act_bf = act_rows.astype(jnp.bfloat16)
    kept_all = lax.all_gather(
        jnp.concatenate([joined, h2_bf, act_bf], axis=1), "wa", axis=0, tiled=True
    )
    out_rows = (x_mid + jnp.dot(act_bf, m_down, preferred_element_type=jnp.float32)).astype(
        jnp.bfloat16
    )
    dy_bf = d_out[0]
    d_act = jnp.dot(dy_bf, m_down.T, preferred_element_type=jnp.float32)
    d_gate_up = act_back(d_act)[0].astype(jnp.bfloat16)
    d_h2 = jnp.dot(d_gate_up, m_gate_up.T, preferred_element_type=jnp.float32)
    d_mid, g_gain_ff = norm_ff_back(d_h2)
    d_mid = d_mid + dy_bf.astype(jnp.float32)
    d_mix = d_mid.astype(jnp.bfloat16)
    d_joined = jnp.dot(d_mix, m_mix_out.T, preferred_element_type=jnp.float32)

    from_out = out_back(d_joined[:, :inner_width])
    lambdas = grads_after(from_out[8], my_decays, ctx_count)

    d_att = (
        d_joined[:, inner_width:].astype(jnp.bfloat16).reshape(row_count, KVHEADS, groups, HEAD_DIM)
    )
    d_term = jnp.transpose(
        jnp.sum(d_att.astype(jnp.float32) * attended.astype(jnp.float32), axis=-1), (1, 2, 0)
    )
    d_prob = jnp.einsum("tgjd,sgd->gjts", d_att, values, preferred_element_type=jnp.float32)
    d_score = (probability * (d_prob - d_term[..., None])).astype(jnp.bfloat16)
    q_grad = (
        jnp.einsum("gjts,sgd->tgjd", d_score, keys, preferred_element_type=jnp.float32)
        * score_scale
    )
    key_grad = (
        jnp.einsum("gjts,tgjd->sgd", d_score, q_rot, preferred_element_type=jnp.float32)
        * score_scale
    )
    value_grad = jnp.einsum("gjts,tgjd->sgd", prob_bf, d_att, preferred_element_type=jnp.float32)
    own_kv_grad = lax.psum_scatter(
        jnp.concatenate(
            [key_grad.reshape(-1, kv_width), value_grad.reshape(-1, kv_width)], axis=1
        ).astype(jnp.bfloat16),
        "ctx",
        scatter_dimension=0,
        tiled=True,
    ).astype(jnp.float32)
    d_q = rotate(q_grad.reshape(row_count, QHEADS, HEAD_DIM), positions, -1.0).reshape(
        row_count, QHEADS * HEAD_DIM
    )
    d_k = rotate(
        own_kv_grad[:, :kv_width].reshape(row_count, KVHEADS, HEAD_DIM), positions, -1.0
    ).reshape(row_count, kv_width)

    grad_cols = by_columns_of(d_mix, d_gate_up, dy_bf, wa_count)
    cat_width = joined.shape[1]
    model_width = tokens.shape[1]
    g_mix_out = column_grad(kept_all[:, :cat_width], grad_cols[0])
    g_gate_up = column_grad(kept_all[:, cat_width : cat_width + model_width], grad_cols[1])
    g_down = column_grad(kept_all[:, cat_width + model_width :], grad_cols[2])

    d_decay = jnp.sum(lambdas * incoming, axis=(2, 3))
    from_state = states_back((d_decay, lambdas))
    from_inputs = inputs_back(
        (
            from_out[0] + from_state[0],
            from_out[1] + from_state[1],
            from_out[2],
            from_out[3] + from_state[2],
            from_out[4] + from_state[3],
        )
    )
    d_exts, d_dts = from_inputs[0], from_inputs[1]
    rim_grads = extended_2(d_exts[:, :conv_lag].astype(jnp.bfloat16), (("ctx", 0),), 1).astype(
        jnp.float32
    )
    extra_first = rim_grads[3] + jnp.where(at_end, d_exts[1][:conv_lag], 0.0)
    extra_second = rim_grads[0]
    d_xbc_first = d_exts[0][conv_lag:] + jnp.pad(extra_first, ((block_len - conv_lag, 0), (0, 0)))
    d_xbc_second = d_exts[1][conv_lag:] + jnp.pad(extra_second, ((block_len - conv_lag, 0), (0, 0)))
    d_proj = jnp.concatenate(
        [
            from_out[5].astype(jnp.bfloat16),
            jnp.concatenate([d_xbc_first, d_xbc_second], axis=0).astype(jnp.bfloat16),
            d_dts.reshape(row_count, mamba_heads).astype(jnp.bfloat16),
            d_q.astype(jnp.bfloat16),
            d_k.astype(jnp.bfloat16),
            own_kv_grad[:, kv_width:].astype(jnp.bfloat16),
        ],
        axis=1,
    )
    d_proj_cols = by_columns(d_proj)
    g_mix_in = column_grad(h_all, d_proj_cols)
    d_h = lax.psum_scatter(
        jnp.dot(d_proj_cols, w_mix_in.T, preferred_element_type=jnp.float32).astype(jnp.bfloat16),
        "wa",
        scatter_dimension=0,
        tiled=True,
    ).astype(jnp.float32)
    d_x_norm, g_gain_in = norm_in_back(d_h)
    x_grad = d_mid + d_x_norm
    small_parts = (
        g_gain_in,
        from_inputs[2],
        from_inputs[3],
        from_inputs[4],
        from_inputs[5],
        from_out[6],
        from_out[7],
        g_gain_ff,
    )
    flat = jnp.concatenate([part.reshape(-1) for part in small_parts])
    flat = jnp.pad(flat, (0, -flat.shape[0] % 1024)).reshape(-1, 128)
    flat = jnp.sum(lax.all_gather(flat, ("ctx", "wa"), axis=0), axis=0).reshape(-1)
    small = []
    place = 0
    for part in small_parts:
        small.append(flat[place : place + part.size].reshape(part.shape))
        place += part.size
    return (
        out_rows[None],
        x_grad[None],
        small[0],
        g_mix_in,
        small[1],
        small[2],
        small[3],
        small[4],
        small[5],
        small[6],
        g_mix_out,
        small[7],
        g_gate_up,
        g_down,
    )


def solution(mesh):
    in_specs = (
        P("wa", "ctx", None),
        P("wa", None),
        P("wa", "ctx", None),
        P(),
        P(None, "wa"),
        P(),
        P(),
        P(),
        P(),
        P(),
        P(),
        P(None, "wa"),
        P(),
        P(None, "wa"),
        P(None, "wa"),
    )
    out_specs = (
        P("wa", "ctx", None),
        P("wa", "ctx", None),
        P(),
        P("ctx", "wa"),
        P(),
        P(),
        P(),
        P(),
        P(),
        P(),
        P("ctx", "wa"),
        P(),
        P("ctx", "wa"),
        P("ctx", "wa"),
    )
    return jax.shard_map(local, mesh=mesh, in_specs=in_specs, out_specs=out_specs, check_vma=False)
```

```python
import jax
import jax.numpy as jnp
from jax import lax
from jax.sharding import PartitionSpec as P

QHEADS = 8
KVHEADS = 2
HEAD_DIM = 64


EPS = 1e-05
ROPE_BASE = 100000000000.0
HIGH = lax.Precision.HIGH


def extended_2(cells, sides, width):
    for axis, dim in sides:
        count = lax.axis_size(axis)
        ends = count - 1
        head = lax.slice_in_dim(cells, 0, width, axis=dim)
        tail = lax.slice_in_dim(cells, cells.shape[dim] - width, cells.shape[dim], axis=dim)
        cells = jnp.concatenate(
            [
                lax.ppermute(tail, axis, [(i, (i + 1) % count) for i in range(ends)]),
                cells,
                lax.ppermute(head, axis, [((i + 1) % count, i) for i in range(ends)]),
            ],
            axis=dim,
        )
    return cells


def norm_rows(values, gain):
    return values * lax.rsqrt(jnp.mean(values * values, axis=-1, keepdims=True) + EPS) * gain


def swiglu(mixed):
    half_size = mixed.shape[-1] // 2
    return jax.nn.silu(mixed[:, :half_size]) * mixed[:, half_size:]


def rotate(values, positions, direction):
    head_size = values.shape[-1]
    half_size = head_size // 2
    frequency = ROPE_BASE ** (-2.0 * jnp.arange(half_size, dtype=jnp.float32) / head_size)
    angles = positions.astype(jnp.float32)[:, None] * frequency[None, :]
    cosine = jnp.cos(angles)[:, None, :]
    sine_part = direction * jnp.sin(angles)[:, None, :]
    first_half = values[..., :half_size]
    second_half = values[..., half_size:]
    return jnp.concatenate(
        [
            first_half * cosine - second_half * sine_part,
            second_half * cosine + first_half * sine_part,
        ],
        axis=-1,
    )


def conv_rows(extended, seg_ext, conv_w, conv_b):
    conv_lag = conv_w.shape[0] - 1
    length = extended.shape[0] - conv_lag
    summed = jnp.zeros((length, extended.shape[1]), jnp.float32) + conv_b[None, :]
    for tap_index in range(conv_lag + 1):
        same_doc = (seg_ext[tap_index : tap_index + length] == seg_ext[conv_lag:]).astype(
            jnp.float32
        )
        summed = (
            summed
            + conv_w[tap_index][None, :]
            * extended[tap_index : tap_index + length]
            * same_doc[:, None]
        )
    return jax.nn.silu(summed)


def block_inputs(extended, seg_ext, raw_dt, conv_w, conv_b, dt_bias, a_log, inner_width):
    mixed = conv_rows(extended, seg_ext, conv_w, conv_b)
    length = mixed.shape[0]
    mamba_heads = dt_bias.shape[0]
    state_size = (mixed.shape[1] - inner_width) // 2
    inputs_x = mixed[:, :inner_width].reshape(length, mamba_heads, inner_width // mamba_heads)
    b_rows = mixed[:, inner_width : inner_width + state_size]
    c_rows = mixed[:, inner_width + state_size :]
    step_dt = jax.nn.softplus(raw_dt + dt_bias[None, :])
    log_decay = -step_dt * jnp.exp(a_log)[None, :]
    return (inputs_x, b_rows, c_rows, step_dt, log_decay)


def block_state(inputs_x, b_rows, step_dt, log_decay, seg_block, seg_before):
    cumulative = jnp.cumsum(log_decay, axis=0)
    keep_end = (seg_block == seg_block[-1]).astype(jnp.float32)
    weights = jnp.exp(cumulative[-1][None, :] - cumulative) * keep_end[:, None] * step_dt
    end_state = jnp.einsum("shp,sn->hpn", weights[:, :, None] * inputs_x, b_rows, precision=HIGH)
    decay_all = jnp.exp(cumulative[-1]) * (seg_block[-1] == seg_before).astype(jnp.float32)
    return (decay_all, end_state)


def block_output(
    inputs_x, b_rows, c_rows, step_dt, log_decay, d_skip, seg_block, seg_before, state_in
):
    length = inputs_x.shape[0]
    cumulative = jnp.cumsum(log_decay, axis=0)
    lower_tri = jnp.arange(length)[:, None] >= jnp.arange(length)[None, :]
    allowed = lower_tri & (seg_block[:, None] == seg_block[None, :])
    across = cumulative.T
    exponent = jnp.where(allowed[None], across[:, :, None] - across[:, None, :], -jnp.inf)
    intersection = jnp.dot(c_rows, b_rows.T, precision=HIGH)
    mixing = jnp.exp(exponent) * intersection[None] * step_dt.T[:, None, :]
    inner_out = jnp.einsum("hts,shp->thp", mixing, inputs_x, precision=HIGH)
    carried = (seg_block == seg_before).astype(jnp.float32)
    from_state = (
        jnp.einsum("tn,hpn->thp", c_rows, state_in, precision=HIGH)
        * (jnp.exp(cumulative) * carried[:, None])[:, :, None]
    )
    return inner_out + from_state + d_skip[None, :, None] * inputs_x


def gated_norm(outputs, gate_rows, gain_gate):
    return norm_rows(outputs * jax.nn.silu(gate_rows), gain_gate)


def block_chain(states, decays, reverse):
    order = range(states.shape[0])
    order = order[::-1] if reverse else order
    held = jnp.zeros(states.shape[1:], jnp.float32)
    before = [None] * states.shape[0]
    for at in order:
        before[at] = held.astype(jnp.bfloat16)
        held = decays[at][:, None] * held + states[at].astype(jnp.float32)
    return jnp.stack(before)


def swap_blocks(parts):
    return jnp.concatenate([parts[:, 0], parts[::-1, 1]], axis=0)


def unswap_blocks(blocks, count):
    return jnp.stack([blocks[:count], blocks[count:][::-1]], axis=1)


def cut_rows(states, count):
    rows = states.shape[1] * states.shape[2] // count
    cut = states.astype(jnp.bfloat16).reshape(2, count, rows, states.shape[3])
    return jnp.swapaxes(cut, 0, 1)


def join_rows(cut, shape):
    return jnp.swapaxes(cut, 0, 1).reshape(shape).astype(jnp.float32)


def swap_axis(parts):
    return lax.all_to_all(parts, "ctx", split_axis=0, concat_axis=0, tiled=True)


def states_before(states, decays, ctx_count):
    heads, width, size = states.shape[1:]
    rows = heads * width // ctx_count
    cut = cut_rows(states, ctx_count)
    high = decays.astype(jnp.bfloat16)
    low = (decays - high.astype(jnp.float32)).astype(jnp.bfloat16)
    marks = jnp.pad(jnp.stack([high, low], axis=1), ((0, 0), (0, 14), (0, size - heads)))
    marks = jnp.broadcast_to(marks[None], (ctx_count,) + marks.shape)
    got = swap_axis(jnp.concatenate([cut, marks], axis=2))
    all_decays = (got[:, :, rows, :heads].astype(jnp.float32)) + got[:, :, rows + 1, :heads].astype(
        jnp.float32
    )
    all_decays = jnp.repeat(swap_blocks(all_decays), width, axis=1)
    my_decays = lax.dynamic_slice_in_dim(all_decays, lax.axis_index("ctx") * rows, rows, 1)
    before = block_chain(swap_blocks(got[:, :, :rows]), my_decays, False)
    back = swap_axis(unswap_blocks(before, ctx_count))
    return join_rows(back, states.shape), my_decays


def grads_after(grads, my_decays, ctx_count, early):
    got = swap_axis(cut_rows(grads, ctx_count))
    got, early = lax.optimization_barrier((got, early))
    after = block_chain(swap_blocks(got), my_decays, True)
    return join_rows(swap_axis(unswap_blocks(after, ctx_count)), grads.shape), early


def by_columns(cut):
    got = swap_parts(jnp.swapaxes(cut, 0, 1), "wa")
    return got.reshape(-1, cut.shape[2])


def swap_parts(parts, axis):
    return lax.all_to_all(parts, axis, split_axis=0, concat_axis=0, tiled=True)


def everyone(part, axis):
    return swap_parts(jnp.broadcast_to(part[None], (lax.axis_size(axis),) + part.shape), axis)


def sum_parts(values, axis):
    cut = values.astype(jnp.bfloat16).reshape((lax.axis_size(axis), -1) + values.shape[1:])
    return jnp.sum(swap_parts(cut, axis).astype(jnp.float32), axis=0)


def shares(values, count):
    return values.reshape(values.shape[0], count, values.shape[1] // count)


def by_columns_of(first, second, third, count):
    cuts = [shares(first, count), shares(second, count), shares(third, count)]
    joined = jnp.concatenate(cuts, axis=2)
    got = by_columns(joined)
    one = cuts[0].shape[2]
    two = one + cuts[1].shape[2]
    return (got[:, :one], got[:, one:two], got[:, two:])


def column_grad(kept_rows, grad_cols):
    return jnp.einsum(
        "tk,tn->kn", kept_rows, grad_cols, preferred_element_type=jnp.float32
    ).astype(jnp.bfloat16)


def scatter_rows(values):
    return lax.psum_scatter(values, "ctx", scatter_dimension=0, tiled=True).astype(jnp.float32)


def fold_rows(values, rows, count):
    height = rows // count
    fold = values.shape[0] // rows
    cut = values.reshape(count, fold, height, values.shape[1])
    return jnp.swapaxes(cut, 1, 2).reshape(rows, fold * values.shape[1])


def unfold_rows(values, width):
    cut = values.reshape(values.shape[0], -1, width)
    return jnp.swapaxes(cut, 0, 1).reshape(-1, width)


def to_stored(natural, ctx_count):
    tail_shape = natural.shape[1:]
    half_len = natural.shape[0] // 2
    block_len = half_len // ctx_count
    leading = natural[:half_len].reshape((ctx_count, block_len) + tail_shape)
    trailing = natural[half_len:].reshape((ctx_count, block_len) + tail_shape)[::-1]
    return jnp.stack([leading, trailing], axis=1).reshape(natural.shape)


def local(
    x_in,
    seg_ids,
    d_out,
    gain_in,
    w_mix_in,
    conv_w,
    conv_b,
    dt_bias,
    a_log,
    d_skip,
    gain_gate,
    w_mix_out,
    gain_ff,
    w_gate_up,
    w_down,
):
    ctx_count = lax.axis_size("ctx")
    wa_count = lax.axis_size("wa")
    ctx_place = lax.axis_index("ctx")
    at_end = ctx_place == ctx_count - 1
    tokens = x_in[0]
    row_count = tokens.shape[0]
    block_len = row_count // 2
    seg_all = seg_ids[0]
    inner_width = gain_gate.shape[0]
    conv_width = conv_w.shape[1]
    mamba_heads = dt_bias.shape[0]
    conv_lag = conv_w.shape[0] - 1
    groups = QHEADS // KVHEADS
    score_scale = HEAD_DIM ** (-0.5)
    starts = (ctx_place * block_len, (2 * ctx_count - 1 - ctx_place) * block_len)
    offsets = jnp.arange(block_len, dtype=jnp.int32)
    positions = jnp.concatenate([starts[0] + offsets, starts[1] + offsets])
    x_rows = tokens.astype(jnp.float32)
    h_rows, norm_in_back = jax.vjp(norm_rows, x_rows, gain_in)
    h_all = lax.all_gather(h_rows.astype(jnp.bfloat16), "wa", axis=0, tiled=True)
    proj_cols = jnp.dot(h_all, w_mix_in, preferred_element_type=jnp.float32).astype(jnp.bfloat16)
    proj = lax.all_to_all(proj_cols, "wa", split_axis=0, concat_axis=1, tiled=True)
    proj = lax.optimization_barrier(proj)
    m_mix_out = lax.all_gather(w_mix_out, "wa", axis=1, tiled=True)
    m_down = lax.all_gather(w_down, "wa", axis=1, tiled=True)
    m_gate_up = lax.all_gather(w_gate_up, "wa", axis=1, tiled=True)
    col_q = inner_width + conv_width + mamba_heads
    col_k = col_q + QHEADS * HEAD_DIM
    col_v = col_k + KVHEADS * HEAD_DIM
    kv_width = KVHEADS * HEAD_DIM
    gate_part = proj[:, :inner_width].astype(jnp.float32)
    xbc_part = proj[:, inner_width : inner_width + conv_width]
    dt_part = proj[:, inner_width + conv_width : col_q].astype(jnp.float32)
    q_rot = rotate(
        proj[:, col_q:col_k].astype(jnp.float32).reshape(row_count, QHEADS, HEAD_DIM),
        positions,
        1.0,
    ).astype(jnp.bfloat16)
    q_rot = q_rot.reshape(row_count, KVHEADS, groups, HEAD_DIM)
    k_rot = rotate(
        proj[:, col_k:col_v].astype(jnp.float32).reshape(row_count, KVHEADS, HEAD_DIM),
        positions,
        1.0,
    ).astype(jnp.bfloat16)
    kv_own = jnp.concatenate([k_rot.reshape(row_count, kv_width), proj[:, col_v:]], axis=1)
    kv_all = everyone(kv_own, "ctx").reshape(-1, 2 * kv_width)
    tails = (xbc_part[block_len - conv_lag : block_len], xbc_part[row_count - conv_lag :])
    rim = extended_2(jnp.stack([tails[1], tails[0]]), (("ctx", 0),), 1)
    previous = (rim[0], jnp.where(at_end, tails[0], rim[3]))
    seg_exts = []
    seg_befores = []
    extendeds = []
    for part_index in range(2):
        low_row = part_index * block_len
        index_ext = (
            starts[part_index] - conv_lag + jnp.arange(block_len + conv_lag, dtype=jnp.int32)
        )
        seg_exts.append(jnp.where(index_ext >= 0, jnp.take(seg_all, jnp.maximum(index_ext, 0)), -1))
        seg_befores.append(jnp.take(seg_all, jnp.maximum(starts[part_index] - 1, 0)))
        extendeds.append(
            jnp.concatenate(
                [previous[part_index], xbc_part[low_row : low_row + block_len]], axis=0
            ).astype(jnp.float32)
        )
    seg_ext = jnp.stack(seg_exts)
    seg_before = jnp.stack(seg_befores)
    seg_block = seg_ext[:, conv_lag:]

    def all_inputs(extended, raw_dt, conv_w, conv_b, dt_bias, a_log):
        return jax.vmap(
            lambda ext, seg, raw: block_inputs(
                ext, seg, raw, conv_w, conv_b, dt_bias, a_log, inner_width
            )
        )(extended, seg_ext, raw_dt)

    def all_states(inputs_x, b_rows, step_dt, log_decay):
        return jax.vmap(block_state)(inputs_x, b_rows, step_dt, log_decay, seg_block, seg_before)

    def all_outputs(
        inputs_x, b_rows, c_rows, step_dt, log_decay, gate_rows, d_skip, gain_gate, state_in
    ):
        outputs = jax.vmap(block_output, in_axes=(0, 0, 0, 0, 0, None, 0, 0, 0))(
            inputs_x, b_rows, c_rows, step_dt, log_decay, d_skip, seg_block, seg_before, state_in
        )
        return gated_norm(outputs.reshape(row_count, inner_width), gate_rows, gain_gate)

    (inputs_x, b_rows, c_rows, step_dt, log_decay), inputs_back = jax.vjp(
        all_inputs,
        jnp.stack(extendeds),
        dt_part.reshape(2, block_len, mamba_heads),
        conv_w,
        conv_b,
        dt_bias,
        a_log,
    )
    (decays, states), states_back = jax.vjp(all_states, inputs_x, b_rows, step_dt, log_decay)
    incoming, my_decays = states_before(states, decays, ctx_count)

    keys = kv_all[:, :kv_width].reshape(-1, KVHEADS, HEAD_DIM)
    values = kv_all[:, kv_width:].reshape(-1, KVHEADS, HEAD_DIM)
    key_seg = to_stored(seg_all, ctx_count)
    key_pos = to_stored(jnp.arange(seg_all.shape[0], dtype=jnp.int32), ctx_count)
    query_seg = seg_block.reshape(row_count)
    allowed = (key_pos[None, :] <= positions[:, None]) & (key_seg[None, :] == query_seg[:, None])
    scores = (
        jnp.einsum("tgjd,sgd->gjts", q_rot, keys, preferred_element_type=jnp.float32) * score_scale
    )
    row_max = jnp.max(jnp.where(allowed, scores, -1e30), axis=-1, keepdims=True)
    raised = jnp.where(allowed, jnp.exp(scores - row_max), 0.0)
    probability = raised * (1.0 / jnp.sum(raised, axis=-1, keepdims=True))
    prob_bf = probability.astype(jnp.bfloat16)
    attended = jnp.einsum(
        "gjts,sgd->tgjd", prob_bf, values, preferred_element_type=jnp.float32
    ).astype(jnp.bfloat16)

    mamba_out, out_back = jax.vjp(
        all_outputs,
        inputs_x,
        b_rows,
        c_rows,
        step_dt,
        log_decay,
        gate_part,
        d_skip,
        gain_gate,
        incoming,
    )
    joined = jnp.concatenate(
        [mamba_out.astype(jnp.bfloat16), attended.reshape(row_count, QHEADS * HEAD_DIM)], axis=1
    )
    x_mid = x_rows + jnp.dot(joined, m_mix_out, preferred_element_type=jnp.float32)
    h2_rows, norm_ff_back = jax.vjp(norm_rows, x_mid, gain_ff)
    h2_bf = h2_rows.astype(jnp.bfloat16)
    gate_up = jnp.dot(h2_bf, m_gate_up, preferred_element_type=jnp.float32)
    act_rows, act_back = jax.vjp(swiglu, gate_up)
    act_bf = act_rows.astype(jnp.bfloat16)
    kept_all = lax.all_gather(
        jnp.concatenate([joined, h2_bf, act_bf], axis=1), "wa", axis=0, tiled=True
    )
    out_rows = (x_mid + jnp.dot(act_bf, m_down, preferred_element_type=jnp.float32)).astype(
        jnp.bfloat16
    )
    dy_bf = d_out[0]
    d_act = jnp.dot(dy_bf, m_down.T, preferred_element_type=jnp.float32)
    d_gate_up = act_back(d_act)[0].astype(jnp.bfloat16)
    d_h2 = jnp.dot(d_gate_up, m_gate_up.T, preferred_element_type=jnp.float32)
    d_mid, g_gain_ff = norm_ff_back(d_h2)
    d_mid = d_mid + dy_bf.astype(jnp.float32)
    d_mix = d_mid.astype(jnp.bfloat16)
    d_joined = jnp.dot(d_mix, m_mix_out.T, preferred_element_type=jnp.float32)

    from_out = out_back(d_joined[:, :inner_width])
    grad_cols = by_columns_of(d_mix, d_gate_up, dy_bf, wa_count)
    cat_width = joined.shape[1]
    model_width = tokens.shape[1]
    early = jnp.concatenate(
        [
            fold_rows(column_grad(kept_all[:, :cat_width], grad_cols[0]), model_width, ctx_count),
            column_grad(kept_all[:, cat_width : cat_width + model_width], grad_cols[1]),
            fold_rows(
                column_grad(kept_all[:, cat_width + model_width :], grad_cols[2]),
                model_width,
                ctx_count,
            ),
        ],
        axis=1,
    )
    lambdas, early = grads_after(from_out[8], my_decays, ctx_count, early)
    early = scatter_rows(early)
    mix_end = cat_width // model_width * w_mix_out.shape[1]
    gate_end = mix_end + w_gate_up.shape[1]
    g_mix_out = unfold_rows(early[:, :mix_end], w_mix_out.shape[1])
    g_gate_up = early[:, mix_end:gate_end]
    g_down = unfold_rows(early[:, gate_end:], w_down.shape[1])

    d_att = (
        d_joined[:, inner_width:].astype(jnp.bfloat16).reshape(row_count, KVHEADS, groups, HEAD_DIM)
    )
    d_term = jnp.transpose(
        jnp.sum(d_att.astype(jnp.float32) * attended.astype(jnp.float32), axis=-1), (1, 2, 0)
    )
    d_prob = jnp.einsum("tgjd,sgd->gjts", d_att, values, preferred_element_type=jnp.float32)
    d_score = (probability * (d_prob - d_term[..., None])).astype(jnp.bfloat16)
    q_grad = (
        jnp.einsum("gjts,sgd->tgjd", d_score, keys, preferred_element_type=jnp.float32)
        * score_scale
    )
    key_grad = (
        jnp.einsum("gjts,tgjd->sgd", d_score, q_rot, preferred_element_type=jnp.float32)
        * score_scale
    )
    value_grad = jnp.einsum("gjts,tgjd->sgd", prob_bf, d_att, preferred_element_type=jnp.float32)
    own_kv_grad = sum_parts(
        jnp.concatenate(
            [key_grad.reshape(-1, kv_width), value_grad.reshape(-1, kv_width)], axis=1
        ),
        "ctx",
    )
    d_q = rotate(q_grad.reshape(row_count, QHEADS, HEAD_DIM), positions, -1.0).reshape(
        row_count, QHEADS * HEAD_DIM
    )
    d_k = rotate(
        own_kv_grad[:, :kv_width].reshape(row_count, KVHEADS, HEAD_DIM), positions, -1.0
    ).reshape(row_count, kv_width)

    d_decay = jnp.sum(lambdas * incoming, axis=(2, 3))
    from_state = states_back((d_decay, lambdas))
    from_inputs = inputs_back(
        (
            from_out[0] + from_state[0],
            from_out[1] + from_state[1],
            from_out[2],
            from_out[3] + from_state[2],
            from_out[4] + from_state[3],
        )
    )
    d_exts, d_dts = from_inputs[0], from_inputs[1]
    rim_grads = extended_2(d_exts[:, :conv_lag].astype(jnp.bfloat16), (("ctx", 0),), 1).astype(
        jnp.float32
    )
    extra_first = rim_grads[3] + jnp.where(at_end, d_exts[1][:conv_lag], 0.0)
    extra_second = rim_grads[0]
    d_xbc_first = d_exts[0][conv_lag:] + jnp.pad(extra_first, ((block_len - conv_lag, 0), (0, 0)))
    d_xbc_second = d_exts[1][conv_lag:] + jnp.pad(extra_second, ((block_len - conv_lag, 0), (0, 0)))
    d_proj = jnp.concatenate(
        [
            from_out[5].astype(jnp.bfloat16),
            jnp.concatenate([d_xbc_first, d_xbc_second], axis=0).astype(jnp.bfloat16),
            d_dts.reshape(row_count, mamba_heads).astype(jnp.bfloat16),
            d_q.astype(jnp.bfloat16),
            d_k.astype(jnp.bfloat16),
            own_kv_grad[:, kv_width:].astype(jnp.bfloat16),
        ],
        axis=1,
    )
    d_proj_cols = by_columns(shares(d_proj, wa_count))
    g_mix_in = scatter_rows(column_grad(h_all, d_proj_cols))
    d_h = sum_parts(
        jnp.dot(d_proj_cols, w_mix_in.T, preferred_element_type=jnp.float32), "wa"
    )
    d_x_norm, g_gain_in = norm_in_back(d_h)
    x_grad = d_mid + d_x_norm
    small_parts = (
        g_gain_in,
        from_inputs[2],
        from_inputs[3],
        from_inputs[4],
        from_inputs[5],
        from_out[6],
        from_out[7],
        g_gain_ff,
    )
    flat = jnp.concatenate([part.reshape(-1) for part in small_parts])
    flat = jnp.pad(flat, (0, -flat.shape[0] % 1024)).reshape(-1, 128)
    flat = jnp.sum(everyone(flat, "wa"), axis=0)
    flat = jnp.sum(everyone(flat, "ctx"), axis=0).reshape(-1)
    small = []
    place = 0
    for part in small_parts:
        small.append(flat[place : place + part.size].reshape(part.shape))
        place += part.size
    return (
        out_rows[None],
        x_grad[None],
        small[0],
        g_mix_in,
        small[1],
        small[2],
        small[3],
        small[4],
        small[5],
        small[6],
        g_mix_out,
        small[7],
        g_gate_up,
        g_down,
    )


def solution(mesh):
    in_specs = (
        P("wa", "ctx", None),
        P("wa", None),
        P("wa", "ctx", None),
        P(),
        P(None, "wa"),
        P(),
        P(),
        P(),
        P(),
        P(),
        P(),
        P(None, "wa"),
        P(),
        P(None, "wa"),
        P(None, "wa"),
    )
    out_specs = (
        P("wa", "ctx", None),
        P("wa", "ctx", None),
        P(),
        P("ctx", "wa"),
        P(),
        P(),
        P(),
        P(),
        P(),
        P(),
        P("ctx", "wa"),
        P(),
        P("ctx", "wa"),
        P("ctx", "wa"),
    )
    return jax.shard_map(local, mesh=mesh, in_specs=in_specs, out_specs=out_specs, check_vma=False)
```

```python
import jax
import jax.numpy as jnp
from jax import lax
from jax.sharding import PartitionSpec as P

QHEADS = 8
KVHEADS = 2
HEAD_DIM = 64


EPS = 1e-05
ROPE_BASE = 100000000000.0
STATE_PRECISION = lax.Precision.DEFAULT


def extended_2(cells, sides, width):
    for axis, dim in sides:
        count = lax.axis_size(axis)
        ends = count - 1
        head = lax.slice_in_dim(cells, 0, width, axis=dim)
        tail = lax.slice_in_dim(cells, cells.shape[dim] - width, cells.shape[dim], axis=dim)
        cells = jnp.concatenate(
            [
                lax.ppermute(tail, axis, [(i, (i + 1) % count) for i in range(ends)]),
                cells,
                lax.ppermute(head, axis, [((i + 1) % count, i) for i in range(ends)]),
            ],
            axis=dim,
        )
    return cells


def norm_rows(values, gain):
    return values * lax.rsqrt(jnp.mean(values * values, axis=-1, keepdims=True) + EPS) * gain


def swiglu(mixed):
    half_size = mixed.shape[-1] // 2
    return jax.nn.silu(mixed[:, :half_size]) * mixed[:, half_size:]


def rotate(values, positions, direction):
    head_size = values.shape[-1]
    half_size = head_size // 2
    frequency = ROPE_BASE ** (-2.0 * jnp.arange(half_size, dtype=jnp.float32) / head_size)
    angles = positions.astype(jnp.float32)[:, None] * frequency[None, :]
    cosine = jnp.cos(angles)[:, None, :]
    sine_part = direction * jnp.sin(angles)[:, None, :]
    first_half = values[..., :half_size]
    second_half = values[..., half_size:]
    return jnp.concatenate(
        [
            first_half * cosine - second_half * sine_part,
            second_half * cosine + first_half * sine_part,
        ],
        axis=-1,
    )


def conv_rows(extended, seg_ext, conv_w, conv_b):
    conv_lag = conv_w.shape[0] - 1
    length = extended.shape[0] - conv_lag
    summed = jnp.zeros((length, extended.shape[1]), jnp.float32) + conv_b[None, :]
    for tap_index in range(conv_lag + 1):
        same_doc = (seg_ext[tap_index : tap_index + length] == seg_ext[conv_lag:]).astype(
            jnp.float32
        )
        summed = (
            summed
            + conv_w[tap_index][None, :]
            * extended[tap_index : tap_index + length]
            * same_doc[:, None]
        )
    return jax.nn.silu(summed)


def block_inputs(extended, seg_ext, raw_dt, conv_w, conv_b, dt_bias, a_log, inner_width):
    mixed = conv_rows(extended, seg_ext, conv_w, conv_b)
    length = mixed.shape[0]
    mamba_heads = dt_bias.shape[0]
    state_size = (mixed.shape[1] - inner_width) // 2
    inputs_x = mixed[:, :inner_width].reshape(length, mamba_heads, inner_width // mamba_heads)
    b_rows = mixed[:, inner_width : inner_width + state_size]
    c_rows = mixed[:, inner_width + state_size :]
    step_dt = jax.nn.softplus(raw_dt + dt_bias[None, :])
    log_decay = -step_dt * jnp.exp(a_log)[None, :]
    return (inputs_x, b_rows, c_rows, step_dt, log_decay)


def block_state(inputs_x, b_rows, step_dt, log_decay, seg_block, seg_before):
    cumulative = jnp.cumsum(log_decay, axis=0)
    keep_end = (seg_block == seg_block[-1]).astype(jnp.float32)
    weights = jnp.exp(cumulative[-1][None, :] - cumulative) * keep_end[:, None] * step_dt
    end_state = jnp.einsum("shp,sn->hpn", weights[:, :, None] * inputs_x, b_rows, precision=STATE_PRECISION)
    decay_all = jnp.exp(cumulative[-1]) * (seg_block[-1] == seg_before).astype(jnp.float32)
    return (decay_all, end_state)


def block_output(
    inputs_x, b_rows, c_rows, step_dt, log_decay, d_skip, seg_block, seg_before, state_in
):
    length = inputs_x.shape[0]
    cumulative = jnp.cumsum(log_decay, axis=0)
    lower_tri = jnp.arange(length)[:, None] >= jnp.arange(length)[None, :]
    allowed = lower_tri & (seg_block[:, None] == seg_block[None, :])
    across = cumulative.T
    exponent = jnp.where(allowed[None], across[:, :, None] - across[:, None, :], -jnp.inf)
    intersection = jnp.dot(c_rows, b_rows.T, precision=STATE_PRECISION)
    mixing = jnp.exp(exponent) * intersection[None] * step_dt.T[:, None, :]
    inner_out = jnp.einsum("hts,shp->thp", mixing, inputs_x, precision=STATE_PRECISION)
    carried = (seg_block == seg_before).astype(jnp.float32)
    from_state = (
        jnp.einsum("tn,hpn->thp", c_rows, state_in, precision=STATE_PRECISION)
        * (jnp.exp(cumulative) * carried[:, None])[:, :, None]
    )
    return inner_out + from_state + d_skip[None, :, None] * inputs_x


def gated_norm(outputs, gate_rows, gain_gate):
    return norm_rows(outputs * jax.nn.silu(gate_rows), gain_gate)


def block_chain(states, decays, reverse):
    order = range(states.shape[0])
    order = order[::-1] if reverse else order
    held = jnp.zeros(states.shape[1:], jnp.float32)
    before = [None] * states.shape[0]
    for at in order:
        before[at] = held.astype(jnp.bfloat16)
        held = decays[at][:, None] * held + states[at].astype(jnp.float32)
    return jnp.stack(before)


def swap_blocks(parts):
    return jnp.concatenate([parts[:, 0], parts[::-1, 1]], axis=0)


def unswap_blocks(blocks, count):
    return jnp.stack([blocks[:count], blocks[count:][::-1]], axis=1)


def cut_rows(states, count):
    rows = states.shape[1] * states.shape[2] // count
    cut = states.astype(jnp.bfloat16).reshape(2, count, rows, states.shape[3])
    return jnp.swapaxes(cut, 0, 1)


def join_rows(cut, shape):
    return jnp.swapaxes(cut, 0, 1).reshape(shape).astype(jnp.float32)


def swap_axis(parts):
    return lax.all_to_all(parts, "ctx", split_axis=0, concat_axis=0, tiled=True)


def states_before(states, decays, ctx_count):
    heads, width, size = states.shape[1:]
    rows = heads * width // ctx_count
    cut = cut_rows(states, ctx_count)
    high = decays.astype(jnp.bfloat16)
    low = (decays - high.astype(jnp.float32)).astype(jnp.bfloat16)
    marks = jnp.pad(jnp.stack([high, low], axis=1), ((0, 0), (0, 14), (0, size - heads)))
    marks = jnp.broadcast_to(marks[None], (ctx_count,) + marks.shape)
    got = swap_axis(jnp.concatenate([cut, marks], axis=2))
    all_decays = (got[:, :, rows, :heads].astype(jnp.float32)) + got[:, :, rows + 1, :heads].astype(
        jnp.float32
    )
    all_decays = jnp.repeat(swap_blocks(all_decays), width, axis=1)
    my_decays = lax.dynamic_slice_in_dim(all_decays, lax.axis_index("ctx") * rows, rows, 1)
    before = block_chain(swap_blocks(got[:, :, :rows]), my_decays, False)
    back = swap_axis(unswap_blocks(before, ctx_count))
    return join_rows(back, states.shape), my_decays


def grads_after(grads, my_decays, ctx_count, early):
    got = swap_axis(cut_rows(grads, ctx_count))
    got, early = lax.optimization_barrier((got, early))
    after = block_chain(swap_blocks(got), my_decays, True)
    return join_rows(swap_axis(unswap_blocks(after, ctx_count)), grads.shape), early


def by_columns(cut):
    got = swap_parts(jnp.swapaxes(cut, 0, 1), "wa")
    return got.reshape(-1, cut.shape[2])


def swap_parts(parts, axis):
    return lax.all_to_all(parts, axis, split_axis=0, concat_axis=0, tiled=True)


def everyone(part, axis):
    return swap_parts(jnp.broadcast_to(part[None], (lax.axis_size(axis),) + part.shape), axis)


def sum_parts(values, axis):
    cut = values.astype(jnp.bfloat16).reshape((lax.axis_size(axis), -1) + values.shape[1:])
    return jnp.sum(swap_parts(cut, axis).astype(jnp.float32), axis=0)


def shares(values, count):
    return values.reshape(values.shape[0], count, values.shape[1] // count)


def by_columns_of(first, second, third, count):
    cuts = [shares(first, count), shares(second, count), shares(third, count)]
    joined = jnp.concatenate(cuts, axis=2)
    got = by_columns(joined)
    one = cuts[0].shape[2]
    two = one + cuts[1].shape[2]
    return (got[:, :one], got[:, one:two], got[:, two:])


def column_grad(kept_rows, grad_cols):
    return jnp.einsum(
        "tk,tn->kn", kept_rows, grad_cols, preferred_element_type=jnp.float32
    ).astype(jnp.bfloat16)


def scatter_rows(values):
    return lax.psum_scatter(values, "ctx", scatter_dimension=0, tiled=True)


def fold_rows(values, rows, count):
    height = rows // count
    fold = values.shape[0] // rows
    cut = values.reshape(count, fold, height, values.shape[1])
    return jnp.swapaxes(cut, 1, 2).reshape(rows, fold * values.shape[1])


def unfold_rows(values, width):
    cut = values.reshape(values.shape[0], -1, width)
    return jnp.swapaxes(cut, 0, 1).reshape(-1, width)


def to_stored(natural, ctx_count):
    tail_shape = natural.shape[1:]
    half_len = natural.shape[0] // 2
    block_len = half_len // ctx_count
    leading = natural[:half_len].reshape((ctx_count, block_len) + tail_shape)
    trailing = natural[half_len:].reshape((ctx_count, block_len) + tail_shape)[::-1]
    return jnp.stack([leading, trailing], axis=1).reshape(natural.shape)


def local(
    x_in,
    seg_ids,
    d_out,
    gain_in,
    w_mix_in,
    conv_w,
    conv_b,
    dt_bias,
    a_log,
    d_skip,
    gain_gate,
    w_mix_out,
    gain_ff,
    w_gate_up,
    w_down,
):
    ctx_count = lax.axis_size("ctx")
    wa_count = lax.axis_size("wa")
    ctx_place = lax.axis_index("ctx")
    at_end = ctx_place == ctx_count - 1
    tokens = x_in[0]
    row_count = tokens.shape[0]
    block_len = row_count // 2
    seg_all = seg_ids[0]
    inner_width = gain_gate.shape[0]
    conv_width = conv_w.shape[1]
    mamba_heads = dt_bias.shape[0]
    conv_lag = conv_w.shape[0] - 1
    groups = QHEADS // KVHEADS
    score_scale = HEAD_DIM ** (-0.5)
    starts = (ctx_place * block_len, (2 * ctx_count - 1 - ctx_place) * block_len)
    offsets = jnp.arange(block_len, dtype=jnp.int32)
    positions = jnp.concatenate([starts[0] + offsets, starts[1] + offsets])
    x_rows = tokens.astype(jnp.float32)
    h_rows, norm_in_back = jax.vjp(norm_rows, x_rows, gain_in)
    h_all = lax.all_gather(h_rows.astype(jnp.bfloat16), "wa", axis=0, tiled=True)
    proj_cols = jnp.dot(h_all, w_mix_in, preferred_element_type=jnp.float32).astype(jnp.bfloat16)
    proj = lax.all_to_all(proj_cols, "wa", split_axis=0, concat_axis=1, tiled=True)
    proj = lax.optimization_barrier(proj)
    m_mix_out = lax.all_gather(w_mix_out, "wa", axis=1, tiled=True)
    m_down = lax.all_gather(w_down, "wa", axis=1, tiled=True)
    m_gate_up = lax.all_gather(w_gate_up, "wa", axis=1, tiled=True)
    col_q = inner_width + conv_width + mamba_heads
    col_k = col_q + QHEADS * HEAD_DIM
    col_v = col_k + KVHEADS * HEAD_DIM
    kv_width = KVHEADS * HEAD_DIM
    gate_part = proj[:, :inner_width].astype(jnp.float32)
    xbc_part = proj[:, inner_width : inner_width + conv_width]
    dt_part = proj[:, inner_width + conv_width : col_q].astype(jnp.float32)
    q_rot = rotate(
        proj[:, col_q:col_k].astype(jnp.float32).reshape(row_count, QHEADS, HEAD_DIM),
        positions,
        1.0,
    ).astype(jnp.bfloat16)
    q_rot = q_rot.reshape(row_count, KVHEADS, groups, HEAD_DIM)
    k_rot = rotate(
        proj[:, col_k:col_v].astype(jnp.float32).reshape(row_count, KVHEADS, HEAD_DIM),
        positions,
        1.0,
    ).astype(jnp.bfloat16)
    kv_own = jnp.concatenate([k_rot.reshape(row_count, kv_width), proj[:, col_v:]], axis=1)
    kv_all = everyone(kv_own, "ctx").reshape(-1, 2 * kv_width)
    tails = (xbc_part[block_len - conv_lag : block_len], xbc_part[row_count - conv_lag :])
    rim = extended_2(jnp.stack([tails[1], tails[0]]), (("ctx", 0),), 1)
    previous = (rim[0], jnp.where(at_end, tails[0], rim[3]))
    seg_exts = []
    seg_befores = []
    extendeds = []
    for part_index in range(2):
        low_row = part_index * block_len
        index_ext = (
            starts[part_index] - conv_lag + jnp.arange(block_len + conv_lag, dtype=jnp.int32)
        )
        seg_exts.append(jnp.where(index_ext >= 0, jnp.take(seg_all, jnp.maximum(index_ext, 0)), -1))
        seg_befores.append(jnp.take(seg_all, jnp.maximum(starts[part_index] - 1, 0)))
        extendeds.append(
            jnp.concatenate(
                [previous[part_index], xbc_part[low_row : low_row + block_len]], axis=0
            ).astype(jnp.float32)
        )
    seg_ext = jnp.stack(seg_exts)
    seg_before = jnp.stack(seg_befores)
    seg_block = seg_ext[:, conv_lag:]

    def all_inputs(extended, raw_dt, conv_w, conv_b, dt_bias, a_log):
        return jax.vmap(
            lambda ext, seg, raw: block_inputs(
                ext, seg, raw, conv_w, conv_b, dt_bias, a_log, inner_width
            )
        )(extended, seg_ext, raw_dt)

    def all_states(inputs_x, b_rows, step_dt, log_decay):
        return jax.vmap(block_state)(inputs_x, b_rows, step_dt, log_decay, seg_block, seg_before)

    def all_outputs(
        inputs_x, b_rows, c_rows, step_dt, log_decay, gate_rows, d_skip, gain_gate, state_in
    ):
        outputs = jax.vmap(block_output, in_axes=(0, 0, 0, 0, 0, None, 0, 0, 0))(
            inputs_x, b_rows, c_rows, step_dt, log_decay, d_skip, seg_block, seg_before, state_in
        )
        return gated_norm(outputs.reshape(row_count, inner_width), gate_rows, gain_gate)

    (inputs_x, b_rows, c_rows, step_dt, log_decay), inputs_back = jax.vjp(
        all_inputs,
        jnp.stack(extendeds),
        dt_part.reshape(2, block_len, mamba_heads),
        conv_w,
        conv_b,
        dt_bias,
        a_log,
    )
    (decays, states), states_back = jax.vjp(all_states, inputs_x, b_rows, step_dt, log_decay)
    incoming, my_decays = states_before(states, decays, ctx_count)

    keys = kv_all[:, :kv_width].reshape(-1, KVHEADS, HEAD_DIM)
    values = kv_all[:, kv_width:].reshape(-1, KVHEADS, HEAD_DIM)
    key_seg = to_stored(seg_all, ctx_count)
    key_pos = to_stored(jnp.arange(seg_all.shape[0], dtype=jnp.int32), ctx_count)
    query_seg = seg_block.reshape(row_count)
    allowed = (key_pos[None, :] <= positions[:, None]) & (key_seg[None, :] == query_seg[:, None])
    scores = (
        jnp.einsum("tgjd,sgd->gjts", q_rot, keys, preferred_element_type=jnp.float32) * score_scale
    )
    row_max = jnp.max(jnp.where(allowed, scores, -1e30), axis=-1, keepdims=True)
    raised = jnp.where(allowed, jnp.exp(scores - row_max), 0.0)
    probability = raised * (1.0 / jnp.sum(raised, axis=-1, keepdims=True))
    prob_bf = probability.astype(jnp.bfloat16)
    attended = jnp.einsum(
        "gjts,sgd->tgjd", prob_bf, values, preferred_element_type=jnp.float32
    ).astype(jnp.bfloat16)

    mamba_out, out_back = jax.vjp(
        all_outputs,
        inputs_x,
        b_rows,
        c_rows,
        step_dt,
        log_decay,
        gate_part,
        d_skip,
        gain_gate,
        incoming,
    )
    joined = jnp.concatenate(
        [mamba_out.astype(jnp.bfloat16), attended.reshape(row_count, QHEADS * HEAD_DIM)], axis=1
    )
    x_mid = x_rows + jnp.dot(joined, m_mix_out, preferred_element_type=jnp.float32)
    h2_rows, norm_ff_back = jax.vjp(norm_rows, x_mid, gain_ff)
    h2_bf = h2_rows.astype(jnp.bfloat16)
    gate_up = jnp.dot(h2_bf, m_gate_up, preferred_element_type=jnp.float32)
    act_rows, act_back = jax.vjp(swiglu, gate_up)
    act_bf = act_rows.astype(jnp.bfloat16)
    kept_all = lax.all_gather(
        jnp.concatenate([joined, h2_bf, act_bf], axis=1), "wa", axis=0, tiled=True
    )
    out_rows = (x_mid + jnp.dot(act_bf, m_down, preferred_element_type=jnp.float32)).astype(
        jnp.bfloat16
    )
    dy_bf = d_out[0]
    d_act = jnp.dot(dy_bf, m_down.T, preferred_element_type=jnp.float32)
    d_gate_up = act_back(d_act)[0].astype(jnp.bfloat16)
    d_h2 = jnp.dot(d_gate_up, m_gate_up.T, preferred_element_type=jnp.float32)
    d_mid, g_gain_ff = norm_ff_back(d_h2)
    d_mid = d_mid + dy_bf.astype(jnp.float32)
    d_mix = d_mid.astype(jnp.bfloat16)
    d_joined = jnp.dot(d_mix, m_mix_out.T, preferred_element_type=jnp.float32)

    from_out = out_back(d_joined[:, :inner_width])
    grad_cols = by_columns_of(d_mix, d_gate_up, dy_bf, wa_count)
    cat_width = joined.shape[1]
    model_width = tokens.shape[1]
    early = jnp.concatenate(
        [
            fold_rows(column_grad(kept_all[:, :cat_width], grad_cols[0]), model_width, ctx_count),
            column_grad(kept_all[:, cat_width : cat_width + model_width], grad_cols[1]),
            fold_rows(
                column_grad(kept_all[:, cat_width + model_width :], grad_cols[2]),
                model_width,
                ctx_count,
            ),
        ],
        axis=1,
    )
    lambdas, early = grads_after(from_out[8], my_decays, ctx_count, early)
    early = scatter_rows(early)

    d_att = (
        d_joined[:, inner_width:].astype(jnp.bfloat16).reshape(row_count, KVHEADS, groups, HEAD_DIM)
    )
    d_term = jnp.transpose(
        jnp.sum(d_att.astype(jnp.float32) * attended.astype(jnp.float32), axis=-1), (1, 2, 0)
    )
    d_prob = jnp.einsum("tgjd,sgd->gjts", d_att, values, preferred_element_type=jnp.float32)
    d_score = (probability * (d_prob - d_term[..., None])).astype(jnp.bfloat16)
    q_grad = (
        jnp.einsum("gjts,sgd->tgjd", d_score, keys, preferred_element_type=jnp.float32)
        * score_scale
    )
    key_grad = (
        jnp.einsum("gjts,tgjd->sgd", d_score, q_rot, preferred_element_type=jnp.float32)
        * score_scale
    )
    value_grad = jnp.einsum("gjts,tgjd->sgd", prob_bf, d_att, preferred_element_type=jnp.float32)
    own_kv_grad = sum_parts(
        jnp.concatenate(
            [key_grad.reshape(-1, kv_width), value_grad.reshape(-1, kv_width)], axis=1
        ),
        "ctx",
    )
    d_q = rotate(q_grad.reshape(row_count, QHEADS, HEAD_DIM), positions, -1.0).reshape(
        row_count, QHEADS * HEAD_DIM
    )
    d_k = rotate(
        own_kv_grad[:, :kv_width].reshape(row_count, KVHEADS, HEAD_DIM), positions, -1.0
    ).reshape(row_count, kv_width)

    d_decay = jnp.sum(lambdas * incoming, axis=(2, 3))
    from_state = states_back((d_decay, lambdas))
    from_inputs = inputs_back(
        (
            from_out[0] + from_state[0],
            from_out[1] + from_state[1],
            from_out[2],
            from_out[3] + from_state[2],
            from_out[4] + from_state[3],
        )
    )
    d_exts, d_dts = from_inputs[0], from_inputs[1]
    rim_grads = extended_2(d_exts[:, :conv_lag].astype(jnp.bfloat16), (("ctx", 0),), 1).astype(
        jnp.float32
    )
    extra_first = rim_grads[3] + jnp.where(at_end, d_exts[1][:conv_lag], 0.0)
    extra_second = rim_grads[0]
    d_xbc_first = d_exts[0][conv_lag:] + jnp.pad(extra_first, ((block_len - conv_lag, 0), (0, 0)))
    d_xbc_second = d_exts[1][conv_lag:] + jnp.pad(extra_second, ((block_len - conv_lag, 0), (0, 0)))
    d_proj = jnp.concatenate(
        [
            from_out[5].astype(jnp.bfloat16),
            jnp.concatenate([d_xbc_first, d_xbc_second], axis=0).astype(jnp.bfloat16),
            d_dts.reshape(row_count, mamba_heads).astype(jnp.bfloat16),
            d_q.astype(jnp.bfloat16),
            d_k.astype(jnp.bfloat16),
            own_kv_grad[:, kv_width:].astype(jnp.bfloat16),
        ],
        axis=1,
    )
    d_proj_cols = by_columns(shares(d_proj, wa_count))
    late, early = lax.optimization_barrier((column_grad(h_all, d_proj_cols), early))
    g_mix_in = scatter_rows(late).astype(jnp.float32)
    early = early.astype(jnp.float32)
    mix_end = cat_width // model_width * w_mix_out.shape[1]
    gate_end = mix_end + w_gate_up.shape[1]
    g_mix_out = unfold_rows(early[:, :mix_end], w_mix_out.shape[1])
    g_gate_up = early[:, mix_end:gate_end]
    g_down = unfold_rows(early[:, gate_end:], w_down.shape[1])
    d_h = sum_parts(
        jnp.dot(d_proj_cols, w_mix_in.T, preferred_element_type=jnp.float32), "wa"
    )
    d_x_norm, g_gain_in = norm_in_back(d_h)
    x_grad = d_mid + d_x_norm
    small_parts = (
        g_gain_in,
        from_inputs[2],
        from_inputs[3],
        from_inputs[4],
        from_inputs[5],
        from_out[6],
        from_out[7],
        g_gain_ff,
    )
    flat = jnp.concatenate([part.reshape(-1) for part in small_parts])
    flat = jnp.pad(flat, (0, -flat.shape[0] % 1024)).reshape(-1, 128)
    flat = jnp.sum(everyone(flat, "wa"), axis=0)
    flat = jnp.sum(everyone(flat, "ctx"), axis=0).reshape(-1)
    small = []
    place = 0
    for part in small_parts:
        small.append(flat[place : place + part.size].reshape(part.shape))
        place += part.size
    return (
        out_rows[None],
        x_grad[None],
        small[0],
        g_mix_in,
        small[1],
        small[2],
        small[3],
        small[4],
        small[5],
        small[6],
        g_mix_out,
        small[7],
        g_gate_up,
        g_down,
    )


def solution(mesh):
    in_specs = (
        P("wa", "ctx", None),
        P("wa", None),
        P("wa", "ctx", None),
        P(),
        P(None, "wa"),
        P(),
        P(),
        P(),
        P(),
        P(),
        P(),
        P(None, "wa"),
        P(),
        P(None, "wa"),
        P(None, "wa"),
    )
    out_specs = (
        P("wa", "ctx", None),
        P("wa", "ctx", None),
        P(),
        P("ctx", "wa"),
        P(),
        P(),
        P(),
        P(),
        P(),
        P(),
        P("ctx", "wa"),
        P(),
        P("ctx", "wa"),
        P("ctx", "wa"),
    )
    return jax.shard_map(local, mesh=mesh, in_specs=in_specs, out_specs=out_specs, check_vma=False)
```

```python
import jax
import jax.numpy as jnp
from jax import lax
from jax.sharding import PartitionSpec as P

QHEADS = 8
KVHEADS = 2
HEAD_DIM = 64


EPS = 1e-05
ROPE_BASE = 100000000000.0
STATE_PRECISION = lax.Precision.DEFAULT


def extended_2(cells, sides, width):
    for axis, dim in sides:
        count = lax.axis_size(axis)
        ends = count - 1
        head = lax.slice_in_dim(cells, 0, width, axis=dim)
        tail = lax.slice_in_dim(cells, cells.shape[dim] - width, cells.shape[dim], axis=dim)
        cells = jnp.concatenate(
            [
                lax.ppermute(tail, axis, [(i, (i + 1) % count) for i in range(ends)]),
                cells,
                lax.ppermute(head, axis, [((i + 1) % count, i) for i in range(ends)]),
            ],
            axis=dim,
        )
    return cells


def norm_rows(values, gain):
    return values * lax.rsqrt(jnp.mean(values * values, axis=-1, keepdims=True) + EPS) * gain


def swiglu(mixed):
    half_size = mixed.shape[-1] // 2
    return jax.nn.silu(mixed[:, :half_size]) * mixed[:, half_size:]


def rotate(values, positions, direction):
    head_size = values.shape[-1]
    half_size = head_size // 2
    frequency = ROPE_BASE ** (-2.0 * jnp.arange(half_size, dtype=jnp.float32) / head_size)
    angles = positions.astype(jnp.float32)[:, None] * frequency[None, :]
    cosine = jnp.cos(angles)[:, None, :]
    sine_part = direction * jnp.sin(angles)[:, None, :]
    first_half = values[..., :half_size]
    second_half = values[..., half_size:]
    return jnp.concatenate(
        [
            first_half * cosine - second_half * sine_part,
            second_half * cosine + first_half * sine_part,
        ],
        axis=-1,
    )


def conv_rows(extended, seg_ext, conv_w, conv_b):
    conv_lag = conv_w.shape[0] - 1
    length = extended.shape[0] - conv_lag
    summed = jnp.zeros((length, extended.shape[1]), jnp.float32) + conv_b[None, :]
    for tap_index in range(conv_lag + 1):
        same_doc = (seg_ext[tap_index : tap_index + length] == seg_ext[conv_lag:]).astype(
            jnp.float32
        )
        summed = (
            summed
            + conv_w[tap_index][None, :]
            * extended[tap_index : tap_index + length]
            * same_doc[:, None]
        )
    return jax.nn.silu(summed)


def block_inputs(extended, seg_ext, raw_dt, conv_w, conv_b, dt_bias, a_log, inner_width):
    mixed = conv_rows(extended, seg_ext, conv_w, conv_b)
    length = mixed.shape[0]
    mamba_heads = dt_bias.shape[0]
    state_size = (mixed.shape[1] - inner_width) // 2
    inputs_x = mixed[:, :inner_width].reshape(length, mamba_heads, inner_width // mamba_heads)
    b_rows = mixed[:, inner_width : inner_width + state_size]
    c_rows = mixed[:, inner_width + state_size :]
    step_dt = jax.nn.softplus(raw_dt + dt_bias[None, :])
    log_decay = -step_dt * jnp.exp(a_log)[None, :]
    return (inputs_x, b_rows, c_rows, step_dt, log_decay)


def block_state(inputs_x, b_rows, step_dt, log_decay, seg_block, seg_before):
    cumulative = jnp.cumsum(log_decay, axis=0)
    keep_end = (seg_block == seg_block[-1]).astype(jnp.float32)
    weights = jnp.exp(cumulative[-1][None, :] - cumulative) * keep_end[:, None] * step_dt
    end_state = jnp.einsum("shp,sn->hpn", weights[:, :, None] * inputs_x, b_rows, precision=STATE_PRECISION)
    decay_all = jnp.exp(cumulative[-1]) * (seg_block[-1] == seg_before).astype(jnp.float32)
    return (decay_all, end_state)


def block_output(
    inputs_x, b_rows, c_rows, step_dt, log_decay, d_skip, seg_block, seg_before, state_in
):
    length = inputs_x.shape[0]
    cumulative = jnp.cumsum(log_decay, axis=0)
    lower_tri = jnp.arange(length)[:, None] >= jnp.arange(length)[None, :]
    allowed = lower_tri & (seg_block[:, None] == seg_block[None, :])
    across = cumulative.T
    exponent = jnp.where(allowed[None], across[:, :, None] - across[:, None, :], -jnp.inf)
    intersection = jnp.dot(c_rows, b_rows.T, precision=STATE_PRECISION)
    mixing = jnp.exp(exponent) * intersection[None] * step_dt.T[:, None, :]
    inner_out = jnp.einsum("hts,shp->thp", mixing, inputs_x, precision=STATE_PRECISION)
    carried = (seg_block == seg_before).astype(jnp.float32)
    from_state = (
        jnp.einsum("tn,hpn->thp", c_rows, state_in, precision=STATE_PRECISION)
        * (jnp.exp(cumulative) * carried[:, None])[:, :, None]
    )
    return inner_out + from_state + d_skip[None, :, None] * inputs_x


def gated_norm(outputs, gate_rows, gain_gate):
    return norm_rows(outputs * jax.nn.silu(gate_rows), gain_gate)


def block_chain(states, decays, reverse):
    order = range(states.shape[0])
    order = order[::-1] if reverse else order
    held = jnp.zeros(states.shape[1:], jnp.float32)
    before = [None] * states.shape[0]
    for at in order:
        before[at] = held.astype(jnp.bfloat16)
        held = decays[at][:, None] * held + states[at].astype(jnp.float32)
    return jnp.stack(before)


def swap_blocks(parts):
    return jnp.concatenate([parts[:, 0], parts[::-1, 1]], axis=0)


def unswap_blocks(blocks, count):
    return jnp.stack([blocks[:count], blocks[count:][::-1]], axis=1)


def cut_rows(states, count):
    rows = states.shape[1] * states.shape[2] // count
    cut = states.astype(jnp.bfloat16).reshape(2, count, rows, states.shape[3])
    return jnp.swapaxes(cut, 0, 1)


def join_rows(cut, shape):
    return jnp.swapaxes(cut, 0, 1).reshape(shape).astype(jnp.float32)


def swap_axis(parts):
    return lax.all_to_all(parts, "ctx", split_axis=0, concat_axis=0, tiled=True)


def states_before(states, decays, ctx_count):
    heads, width, size = states.shape[1:]
    rows = heads * width // ctx_count
    cut = cut_rows(states, ctx_count)
    high = decays.astype(jnp.bfloat16)
    low = (decays - high.astype(jnp.float32)).astype(jnp.bfloat16)
    marks = jnp.pad(jnp.stack([high, low], axis=1), ((0, 0), (0, 14), (0, size - heads)))
    marks = jnp.broadcast_to(marks[None], (ctx_count,) + marks.shape)
    got = swap_axis(jnp.concatenate([cut, marks], axis=2))
    all_decays = (got[:, :, rows, :heads].astype(jnp.float32)) + got[:, :, rows + 1, :heads].astype(
        jnp.float32
    )
    all_decays = jnp.repeat(swap_blocks(all_decays), width, axis=1)
    my_decays = lax.dynamic_slice_in_dim(all_decays, lax.axis_index("ctx") * rows, rows, 1)
    before = block_chain(swap_blocks(got[:, :, :rows]), my_decays, False)
    back = swap_axis(unswap_blocks(before, ctx_count))
    return join_rows(back, states.shape), my_decays


def grads_after(grads, my_decays, ctx_count, early):
    got = swap_axis(cut_rows(grads, ctx_count))
    after = block_chain(swap_blocks(got), my_decays, True)
    back = swap_axis(unswap_blocks(after, ctx_count))
    back, early = lax.optimization_barrier((back, early))
    return join_rows(back, grads.shape), early


def by_columns(cut):
    got = swap_parts(jnp.swapaxes(cut, 0, 1), "wa")
    return got.reshape(-1, cut.shape[2])


def swap_parts(parts, axis):
    return lax.all_to_all(parts, axis, split_axis=0, concat_axis=0, tiled=True)


def everyone(part, axis):
    return swap_parts(jnp.broadcast_to(part[None], (lax.axis_size(axis),) + part.shape), axis)


def sum_parts(values, axis):
    cut = values.astype(jnp.bfloat16).reshape((lax.axis_size(axis), -1) + values.shape[1:])
    return jnp.sum(swap_parts(cut, axis).astype(jnp.float32), axis=0)


def shares(values, count):
    return values.reshape(values.shape[0], count, values.shape[1] // count)


def by_columns_of(first, second, third, count):
    cuts = [shares(first, count), shares(second, count), shares(third, count)]
    joined = jnp.concatenate(cuts, axis=2)
    got = by_columns(joined)
    one = cuts[0].shape[2]
    two = one + cuts[1].shape[2]
    return (got[:, :one], got[:, one:two], got[:, two:])


def column_grad(kept_rows, grad_cols):
    return jnp.einsum(
        "tk,tn->kn", kept_rows, grad_cols, preferred_element_type=jnp.float32
    ).astype(jnp.bfloat16)


def scatter_rows(values):
    return lax.psum_scatter(values, "ctx", scatter_dimension=0, tiled=True)


def fold_rows(values, rows, count):
    height = rows // count
    fold = values.shape[0] // rows
    cut = values.reshape(count, fold, height, values.shape[1])
    return jnp.swapaxes(cut, 1, 2).reshape(rows, fold * values.shape[1])


def unfold_rows(values, width):
    cut = values.reshape(values.shape[0], -1, width)
    return jnp.swapaxes(cut, 0, 1).reshape(-1, width)


def to_stored(natural, ctx_count):
    tail_shape = natural.shape[1:]
    half_len = natural.shape[0] // 2
    block_len = half_len // ctx_count
    leading = natural[:half_len].reshape((ctx_count, block_len) + tail_shape)
    trailing = natural[half_len:].reshape((ctx_count, block_len) + tail_shape)[::-1]
    return jnp.stack([leading, trailing], axis=1).reshape(natural.shape)


def local(
    x_in,
    seg_ids,
    d_out,
    gain_in,
    w_mix_in,
    conv_w,
    conv_b,
    dt_bias,
    a_log,
    d_skip,
    gain_gate,
    w_mix_out,
    gain_ff,
    w_gate_up,
    w_down,
):
    ctx_count = lax.axis_size("ctx")
    wa_count = lax.axis_size("wa")
    ctx_place = lax.axis_index("ctx")
    at_end = ctx_place == ctx_count - 1
    tokens = x_in[0]
    row_count = tokens.shape[0]
    block_len = row_count // 2
    seg_all = seg_ids[0]
    inner_width = gain_gate.shape[0]
    conv_width = conv_w.shape[1]
    mamba_heads = dt_bias.shape[0]
    conv_lag = conv_w.shape[0] - 1
    groups = QHEADS // KVHEADS
    score_scale = HEAD_DIM ** (-0.5)
    starts = (ctx_place * block_len, (2 * ctx_count - 1 - ctx_place) * block_len)
    offsets = jnp.arange(block_len, dtype=jnp.int32)
    positions = jnp.concatenate([starts[0] + offsets, starts[1] + offsets])
    x_rows = tokens.astype(jnp.float32)
    h_rows, norm_in_back = jax.vjp(norm_rows, x_rows, gain_in)
    h_all = lax.all_gather(h_rows.astype(jnp.bfloat16), "wa", axis=0, tiled=True)
    proj_cols = jnp.dot(h_all, w_mix_in, preferred_element_type=jnp.float32).astype(jnp.bfloat16)
    proj = lax.all_to_all(proj_cols, "wa", split_axis=0, concat_axis=1, tiled=True)
    proj = lax.optimization_barrier(proj)
    m_mix_out = lax.all_gather(w_mix_out, "wa", axis=1, tiled=True)
    m_down = lax.all_gather(w_down, "wa", axis=1, tiled=True)
    m_gate_up = lax.all_gather(w_gate_up, "wa", axis=1, tiled=True)
    col_q = inner_width + conv_width + mamba_heads
    col_k = col_q + QHEADS * HEAD_DIM
    col_v = col_k + KVHEADS * HEAD_DIM
    kv_width = KVHEADS * HEAD_DIM
    gate_part = proj[:, :inner_width].astype(jnp.float32)
    xbc_part = proj[:, inner_width : inner_width + conv_width]
    dt_part = proj[:, inner_width + conv_width : col_q].astype(jnp.float32)
    q_rot = rotate(
        proj[:, col_q:col_k].astype(jnp.float32).reshape(row_count, QHEADS, HEAD_DIM),
        positions,
        1.0,
    ).astype(jnp.bfloat16)
    q_rot = q_rot.reshape(row_count, KVHEADS, groups, HEAD_DIM)
    k_rot = rotate(
        proj[:, col_k:col_v].astype(jnp.float32).reshape(row_count, KVHEADS, HEAD_DIM),
        positions,
        1.0,
    ).astype(jnp.bfloat16)
    kv_own = jnp.concatenate([k_rot.reshape(row_count, kv_width), proj[:, col_v:]], axis=1)
    kv_all = everyone(kv_own, "ctx").reshape(-1, 2 * kv_width)
    tails = (xbc_part[block_len - conv_lag : block_len], xbc_part[row_count - conv_lag :])
    rim = extended_2(jnp.stack([tails[1], tails[0]]), (("ctx", 0),), 1)
    previous = (rim[0], jnp.where(at_end, tails[0], rim[3]))
    seg_exts = []
    seg_befores = []
    extendeds = []
    for part_index in range(2):
        low_row = part_index * block_len
        index_ext = (
            starts[part_index] - conv_lag + jnp.arange(block_len + conv_lag, dtype=jnp.int32)
        )
        seg_exts.append(jnp.where(index_ext >= 0, jnp.take(seg_all, jnp.maximum(index_ext, 0)), -1))
        seg_befores.append(jnp.take(seg_all, jnp.maximum(starts[part_index] - 1, 0)))
        extendeds.append(
            jnp.concatenate(
                [previous[part_index], xbc_part[low_row : low_row + block_len]], axis=0
            ).astype(jnp.float32)
        )
    seg_ext = jnp.stack(seg_exts)
    seg_before = jnp.stack(seg_befores)
    seg_block = seg_ext[:, conv_lag:]

    def all_inputs(extended, raw_dt, conv_w, conv_b, dt_bias, a_log):
        return jax.vmap(
            lambda ext, seg, raw: block_inputs(
                ext, seg, raw, conv_w, conv_b, dt_bias, a_log, inner_width
            )
        )(extended, seg_ext, raw_dt)

    def all_states(inputs_x, b_rows, step_dt, log_decay):
        return jax.vmap(block_state)(inputs_x, b_rows, step_dt, log_decay, seg_block, seg_before)

    def all_outputs(
        inputs_x, b_rows, c_rows, step_dt, log_decay, gate_rows, d_skip, gain_gate, state_in
    ):
        outputs = jax.vmap(block_output, in_axes=(0, 0, 0, 0, 0, None, 0, 0, 0))(
            inputs_x, b_rows, c_rows, step_dt, log_decay, d_skip, seg_block, seg_before, state_in
        )
        return gated_norm(outputs.reshape(row_count, inner_width), gate_rows, gain_gate)

    (inputs_x, b_rows, c_rows, step_dt, log_decay), inputs_back = jax.vjp(
        all_inputs,
        jnp.stack(extendeds),
        dt_part.reshape(2, block_len, mamba_heads),
        conv_w,
        conv_b,
        dt_bias,
        a_log,
    )
    (decays, states), states_back = jax.vjp(all_states, inputs_x, b_rows, step_dt, log_decay)
    incoming, my_decays = states_before(states, decays, ctx_count)

    keys = kv_all[:, :kv_width].reshape(-1, KVHEADS, HEAD_DIM)
    values = kv_all[:, kv_width:].reshape(-1, KVHEADS, HEAD_DIM)
    key_seg = to_stored(seg_all, ctx_count)
    key_pos = to_stored(jnp.arange(seg_all.shape[0], dtype=jnp.int32), ctx_count)
    query_seg = seg_block.reshape(row_count)
    allowed = (key_pos[None, :] <= positions[:, None]) & (key_seg[None, :] == query_seg[:, None])
    scores = (
        jnp.einsum("tgjd,sgd->gjts", q_rot, keys, preferred_element_type=jnp.float32) * score_scale
    )
    row_max = jnp.max(jnp.where(allowed, scores, -1e30), axis=-1, keepdims=True)
    raised = jnp.where(allowed, jnp.exp(scores - row_max), 0.0)
    probability = raised * (1.0 / jnp.sum(raised, axis=-1, keepdims=True))
    prob_bf = probability.astype(jnp.bfloat16)
    attended = jnp.einsum(
        "gjts,sgd->tgjd", prob_bf, values, preferred_element_type=jnp.float32
    ).astype(jnp.bfloat16)

    mamba_out, out_back = jax.vjp(
        all_outputs,
        inputs_x,
        b_rows,
        c_rows,
        step_dt,
        log_decay,
        gate_part,
        d_skip,
        gain_gate,
        incoming,
    )
    joined = jnp.concatenate(
        [mamba_out.astype(jnp.bfloat16), attended.reshape(row_count, QHEADS * HEAD_DIM)], axis=1
    )
    x_mid = x_rows + jnp.dot(joined, m_mix_out, preferred_element_type=jnp.float32)
    h2_rows, norm_ff_back = jax.vjp(norm_rows, x_mid, gain_ff)
    h2_bf = h2_rows.astype(jnp.bfloat16)
    gate_up = jnp.dot(h2_bf, m_gate_up, preferred_element_type=jnp.float32)
    act_rows, act_back = jax.vjp(swiglu, gate_up)
    act_bf = act_rows.astype(jnp.bfloat16)
    kept_all = lax.all_gather(
        jnp.concatenate([joined, h2_bf, act_bf], axis=1), "wa", axis=0, tiled=True
    )
    out_rows = (x_mid + jnp.dot(act_bf, m_down, preferred_element_type=jnp.float32)).astype(
        jnp.bfloat16
    )
    dy_bf = d_out[0]
    d_act = jnp.dot(dy_bf, m_down.T, preferred_element_type=jnp.float32)
    d_gate_up = act_back(d_act)[0].astype(jnp.bfloat16)
    d_h2 = jnp.dot(d_gate_up, m_gate_up.T, preferred_element_type=jnp.float32)
    d_mid, g_gain_ff = norm_ff_back(d_h2)
    d_mid = d_mid + dy_bf.astype(jnp.float32)
    d_mix = d_mid.astype(jnp.bfloat16)
    d_joined = jnp.dot(d_mix, m_mix_out.T, preferred_element_type=jnp.float32)

    from_out = out_back(d_joined[:, :inner_width])
    grad_cols = by_columns_of(d_mix, d_gate_up, dy_bf, wa_count)
    cat_width = joined.shape[1]
    model_width = tokens.shape[1]
    early = jnp.concatenate(
        [
            fold_rows(column_grad(kept_all[:, :cat_width], grad_cols[0]), model_width, ctx_count),
            column_grad(kept_all[:, cat_width : cat_width + model_width], grad_cols[1]),
            fold_rows(
                column_grad(kept_all[:, cat_width + model_width :], grad_cols[2]),
                model_width,
                ctx_count,
            ),
        ],
        axis=1,
    )
    lambdas, early = grads_after(from_out[8], my_decays, ctx_count, early)
    early = scatter_rows(early)

    d_att = (
        d_joined[:, inner_width:].astype(jnp.bfloat16).reshape(row_count, KVHEADS, groups, HEAD_DIM)
    )
    d_term = jnp.transpose(
        jnp.sum(d_att.astype(jnp.float32) * attended.astype(jnp.float32), axis=-1), (1, 2, 0)
    )
    d_prob = jnp.einsum("tgjd,sgd->gjts", d_att, values, preferred_element_type=jnp.float32)
    d_score = (probability * (d_prob - d_term[..., None])).astype(jnp.bfloat16)
    q_grad = (
        jnp.einsum("gjts,sgd->tgjd", d_score, keys, preferred_element_type=jnp.float32)
        * score_scale
    )
    key_grad = (
        jnp.einsum("gjts,tgjd->sgd", d_score, q_rot, preferred_element_type=jnp.float32)
        * score_scale
    )
    value_grad = jnp.einsum("gjts,tgjd->sgd", prob_bf, d_att, preferred_element_type=jnp.float32)
    own_kv_grad = sum_parts(
        jnp.concatenate(
            [key_grad.reshape(-1, kv_width), value_grad.reshape(-1, kv_width)], axis=1
        ),
        "ctx",
    )
    d_q = rotate(q_grad.reshape(row_count, QHEADS, HEAD_DIM), positions, -1.0).reshape(
        row_count, QHEADS * HEAD_DIM
    )
    d_k = rotate(
        own_kv_grad[:, :kv_width].reshape(row_count, KVHEADS, HEAD_DIM), positions, -1.0
    ).reshape(row_count, kv_width)

    d_decay = jnp.sum(lambdas * incoming, axis=(2, 3))
    from_state = states_back((d_decay, lambdas))
    from_inputs = inputs_back(
        (
            from_out[0] + from_state[0],
            from_out[1] + from_state[1],
            from_out[2],
            from_out[3] + from_state[2],
            from_out[4] + from_state[3],
        )
    )
    d_exts, d_dts = from_inputs[0], from_inputs[1]
    rim_grads = extended_2(d_exts[:, :conv_lag].astype(jnp.bfloat16), (("ctx", 0),), 1).astype(
        jnp.float32
    )
    extra_first = rim_grads[3] + jnp.where(at_end, d_exts[1][:conv_lag], 0.0)
    extra_second = rim_grads[0]
    d_xbc_first = d_exts[0][conv_lag:] + jnp.pad(extra_first, ((block_len - conv_lag, 0), (0, 0)))
    d_xbc_second = d_exts[1][conv_lag:] + jnp.pad(extra_second, ((block_len - conv_lag, 0), (0, 0)))
    d_proj = jnp.concatenate(
        [
            from_out[5].astype(jnp.bfloat16),
            jnp.concatenate([d_xbc_first, d_xbc_second], axis=0).astype(jnp.bfloat16),
            d_dts.reshape(row_count, mamba_heads).astype(jnp.bfloat16),
            d_q.astype(jnp.bfloat16),
            d_k.astype(jnp.bfloat16),
            own_kv_grad[:, kv_width:].astype(jnp.bfloat16),
        ],
        axis=1,
    )
    d_proj_cols = by_columns(shares(d_proj, wa_count))
    late, early = lax.optimization_barrier((column_grad(h_all, d_proj_cols), early))
    g_mix_in = scatter_rows(late).astype(jnp.float32)
    early = early.astype(jnp.float32)
    mix_end = cat_width // model_width * w_mix_out.shape[1]
    gate_end = mix_end + w_gate_up.shape[1]
    g_mix_out = unfold_rows(early[:, :mix_end], w_mix_out.shape[1])
    g_gate_up = early[:, mix_end:gate_end]
    g_down = unfold_rows(early[:, gate_end:], w_down.shape[1])
    d_h = sum_parts(
        jnp.dot(d_proj_cols, w_mix_in.T, preferred_element_type=jnp.float32), "wa"
    )
    d_x_norm, g_gain_in = norm_in_back(d_h)
    x_grad = d_mid + d_x_norm
    small_parts = (
        g_gain_in,
        from_inputs[2],
        from_inputs[3],
        from_inputs[4],
        from_inputs[5],
        from_out[6],
        from_out[7],
        g_gain_ff,
    )
    flat = jnp.concatenate([part.reshape(-1) for part in small_parts])
    flat = jnp.pad(flat, (0, -flat.shape[0] % 1024)).reshape(-1, 128)
    flat = jnp.sum(everyone(flat, "wa"), axis=0)
    flat = jnp.sum(everyone(flat, "ctx"), axis=0).reshape(-1)
    small = []
    place = 0
    for part in small_parts:
        small.append(flat[place : place + part.size].reshape(part.shape))
        place += part.size
    return (
        out_rows[None],
        x_grad[None],
        small[0],
        g_mix_in,
        small[1],
        small[2],
        small[3],
        small[4],
        small[5],
        small[6],
        g_mix_out,
        small[7],
        g_gate_up,
        g_down,
    )


def solution(mesh):
    in_specs = (
        P("wa", "ctx", None),
        P("wa", None),
        P("wa", "ctx", None),
        P(),
        P(None, "wa"),
        P(),
        P(),
        P(),
        P(),
        P(),
        P(),
        P(None, "wa"),
        P(),
        P(None, "wa"),
        P(None, "wa"),
    )
    out_specs = (
        P("wa", "ctx", None),
        P("wa", "ctx", None),
        P(),
        P("ctx", "wa"),
        P(),
        P(),
        P(),
        P(),
        P(),
        P(),
        P("ctx", "wa"),
        P(),
        P("ctx", "wa"),
        P("ctx", "wa"),
    )
    return jax.shard_map(local, mesh=mesh, in_specs=in_specs, out_specs=out_specs, check_vma=False)
```
